32 devices in a mesh: grp: 2 (over y), seq: 4 (over z), batch: 4 (over x, core).
Axes of the slice: x: 2, y: 2, z: 4, core: 2. Of those that a mesh axis runs over, the one named last changes fastest.
Arguments:
- head_split_gradient: bfloat16 [8, 768, 2048], P(('grp', 'batch'), 'seq'), parts along dimension 0, may hold values from -6 to 6
- first_layer_input: bfloat16 [8, 768, 2048], P(('grp', 'batch'), None, 'seq'), parts along dimension 0, may hold values from -40 to 40
- second_layer_input: bfloat16 [8, 768, 2048], P(('grp', 'batch'), None, 'seq'), parts along dimension 0, may hold values from -40 to 40
- first_layer_weight: bfloat16 [3, 768, 768], replicated, may hold values from -0.125 to 0.125
- second_layer_weight: bfloat16 [3, 768, 768], replicated, may hold values from -0.125 to 0.125
- first_norm_gain: float32 [768], replicated, may hold values from 0.1 to 1.9
- second_norm_gain: float32 [768], replicated, may hold values from 0.1 to 1.9
Outputs:
- input_gradient_total: bfloat16 [8, 768, 2048], P(('grp', 'batch'), None, 'seq'), parts along dimension 0
- first_weight_gradient: float32 [4608, 768], P(('grp', 'seq')), parts along dimension 0
The draws below stay inside these ranges and needn't reach their ends.
There are 2 independent parts, one for each index of `grp`. The reference program is written for one: setup_inputs(seed, part) draws one part's arguments, and reference() takes and returns one part's arrays. A program takes and returns all parts, laid end to end along the dimension named above; an argument that names none is the same for every part. Nothing has to cross between parts.
All inputs are finite; a program needn't handle non-finite values.
Results may differ from the reference program's by a relative error of at most 0.005.
Values may be sent and summed in bfloat16 or wider, within the bound.
A program may use at most 64 MiB of HBM per device.

```python
import math
import jax
import jax.numpy as jnp
from jax import lax

C = 768
DILATION_FIRST = 512
DILATION_SECOND = 1024
BATCH = 4
POS = 2048


def draw_activation(key):
    key_base, key_pos, key_chan = jax.random.split(key, 3)
    base = jax.random.normal(key_base, (BATCH, C, POS), jnp.float32)
    lowest, highest = (0.3, 3.0)
    pos_scale = jnp.exp(jax.random.uniform(key_pos, (BATCH, 1, POS), jnp.float32, math.log(lowest), math.log(highest)))
    chan_scale = jnp.exp(jax.random.uniform(key_chan, (1, C, 1), jnp.float32, math.log(lowest), math.log(highest)))
    return jnp.clip(base * pos_scale * chan_scale, -40.0, 40.0).astype(jnp.bfloat16)


def draw_first_layer_input(key, part):
    return draw_activation(jax.random.fold_in(key, 11))


def draw_second_layer_input(key, part):
    return draw_activation(jax.random.fold_in(key, 23))


def steps_of(stream_key, extent, shards, low, largest):
    gain, own = 1.0, jax.random.fold_in(stream_key, 6)
    for dim, shards_of in shards:
        draws = jnp.exp(jax.random.uniform(jax.random.fold_in(own, dim), (shards_of,), jnp.float32, low / len(shards), largest / len(shards)))
        gain = gain * jnp.repeat(draws, extent[dim] // shards_of).reshape([-1 if axis == dim else 1 for axis in range(len(extent))])
    return gain


def noise(key, dims, width, limit, cuts=(), held_as=jnp.bfloat16):
    values = jax.random.normal(key, dims, jnp.float32) * width
    if len(cuts) > 0:
        values = steps_of(key, dims, cuts, -0.22, 0.18) * values
    return jnp.clip(values, min=-limit, max=limit).astype(held_as)


def setup_inputs(seed: int = 0, part: int = 0) -> dict:
    seeds = jax.random.split(jax.random.key(seed), 8)
    part_splits = jax.random.split(jax.random.fold_in(seeds[7], part), 8)
    head_split_gradient = noise(part_splits[0], (BATCH, C, POS), 1.0, 6.0, ((0, 4), (1, 4)))
    first_layer_input = draw_first_layer_input(jax.random.fold_in(jax.random.fold_in(seeds[7], part), 71), part)
    second_layer_input = draw_second_layer_input(jax.random.fold_in(jax.random.fold_in(seeds[7], part), 71), part)
    first_layer_weight = noise(seeds[3], (3, C, C), (3 * C) ** -0.5, 0.125)
    second_layer_weight = noise(seeds[4], (3, C, C), (3 * C) ** -0.5, 0.125)
    first_norm_gain = jnp.clip(1.0 + 0.18 * jax.random.normal(seeds[5], (C,), jnp.float32), 0.1, 1.9)
    second_norm_gain = jnp.clip(1.0 + 0.18 * jax.random.normal(seeds[6], (C,), jnp.float32), 0.1, 1.9)
    return {"head_split_gradient": head_split_gradient, "first_layer_input": first_layer_input, "second_layer_input": second_layer_input, "first_layer_weight": first_layer_weight, "second_layer_weight": second_layer_weight, "first_norm_gain": first_norm_gain, "second_norm_gain": second_norm_gain}


EPS = 1e-06
SLOPE = math.sqrt(2.0 / math.pi)
CUBIC = 0.044715

def gelu_slope(normed):
    inner = jnp.tanh(SLOPE * (normed + CUBIC * normed * normed * normed))
    return 0.5 * (1.0 + inner) + 0.5 * normed * (1.0 - inner * inner) * SLOPE * (1.0 + 3.0 * CUBIC * normed * normed)

def prepare(inputs, gain_vec):
    xfloat = inputs.astype(jnp.float32)
    meansq = lax.optimization_barrier(jnp.mean(xfloat * xfloat, axis=1, keepdims=True))
    scale = lax.rsqrt(meansq + EPS)
    normed = xfloat * scale * gain_vec[None, :, None]
    gelu_out = jax.nn.gelu(normed, approximate=True).astype(jnp.bfloat16)
    return (xfloat, scale, normed, gelu_out)

def lower_shift(field, offset):
    return jnp.pad(field[:, :, :field.shape[2] - offset], ((0, 0), (0, 0), (offset, 0)))

def upper_shift(field, offset):
    return jnp.pad(field[:, :, offset:], ((0, 0), (0, 0), (0, offset)))

def weight_grad(g_lower, gelu_out, g_upper, grad_out, scale_factor):
    grad_float = grad_out.astype(jnp.float32)
    pieces = [jnp.einsum('bcp,bop->co', tapped.astype(jnp.float32), grad_float) for tapped in (g_lower, gelu_out, g_upper)]
    return jnp.concatenate(pieces, axis=0) * scale_factor

def input_grad(xfloat, scale, normed, gain_vec, weight, grad_out, grad_upper, grad_lower):
    wfloat = weight.astype(jnp.float32)
    dgelu = jnp.einsum('co,bop->bcp', wfloat[0], grad_upper.astype(jnp.float32))
    dgelu = dgelu + jnp.einsum('co,bop->bcp', wfloat[1], grad_out.astype(jnp.float32))
    dgelu = dgelu + jnp.einsum('co,bop->bcp', wfloat[2], grad_lower.astype(jnp.float32))
    dnorm = dgelu * gelu_slope(normed) * gain_vec[None, :, None]
    inner = lax.optimization_barrier(jnp.mean(dnorm * xfloat, axis=1, keepdims=True))
    dinput = scale * dnorm - xfloat * scale * scale * scale * inner
    return (grad_out.astype(jnp.float32) + dinput).astype(jnp.bfloat16)

def reference(head_split_gradient, first_layer_input, second_layer_input, first_layer_weight, second_layer_weight, first_norm_gain, second_norm_gain):
    scale_factor = 1.0 / math.sqrt(BATCH * POS)
    xfloat_two, scale_two, normed_two, gelu_two = prepare(second_layer_input, second_norm_gain)
    middle_gradient = input_grad(xfloat_two, scale_two, normed_two, second_norm_gain, second_layer_weight, head_split_gradient, upper_shift(head_split_gradient, DILATION_SECOND), lower_shift(head_split_gradient, DILATION_SECOND))
    xfloat_one, scale_one, normed_one, gelu_one = prepare(first_layer_input, first_norm_gain)
    input_gradient_total = input_grad(xfloat_one, scale_one, normed_one, first_norm_gain, first_layer_weight, middle_gradient, upper_shift(middle_gradient, DILATION_FIRST), lower_shift(middle_gradient, DILATION_FIRST))
    first_weight_gradient = weight_grad(lower_shift(gelu_one, DILATION_FIRST), gelu_one, upper_shift(gelu_one, DILATION_FIRST), middle_gradient, scale_factor)
    return (input_gradient_total, first_weight_gradient)
```

```python
import functools
import math

import jax
import jax.numpy as jnp
from jax import lax
from jax.experimental import pallas as pl
from jax.experimental.pallas import tpu as pltpu
from jax.sharding import PartitionSpec as P

DILATION_FIRST = 512
DILATION_SECOND = 1024

EPS = 1e-06
SLOPE = math.sqrt(2.0 / math.pi)
CUBIC = 0.044715

F32 = jnp.float32
BF16 = jnp.bfloat16
MESH = pl.DeviceIdType.MESH
CHUNKS = 2
STRIP = 64
BLOCK = 256


def prepare(u_ref, gain_ref, slope_ref, scale_ref, gelu_ref):
    chan, width = u_ref.shape

    def square(step, total):
        rows = pl.ds(pl.multiple_of(step * STRIP, STRIP), STRIP)
        x = u_ref[rows, :].astype(F32)
        return total + jnp.sum(x * x, axis=0, keepdims=True)

    total = lax.fori_loop(0, chan // STRIP, square, jnp.zeros((1, width), F32))
    scale = lax.rsqrt(total / chan + EPS)
    scale_ref[...] = scale

    @pl.loop(0, chan // STRIP)
    def _(step):
        rows = pl.ds(pl.multiple_of(step * STRIP, STRIP), STRIP)
        gain = gain_ref[rows, :]
        a = u_ref[rows, :].astype(F32) * scale * gain
        t = jnp.tanh(SLOPE * (a + CUBIC * a * a * a))
        slope = 0.5 * (1.0 + t) + 0.5 * a * (1.0 - t * t) * SLOPE * (1.0 + 3.0 * CUBIC * a * a)
        slope_ref[rows, :] = slope * gain
        if gelu_ref is not None:
            gelu_ref[rows, :] = (0.5 * a * (1.0 + t)).astype(BF16)


def layer(w_ref, e_ref, has_low, has_up, cols, u_ref, slope_ref, scale_ref, dg_ref, store):
    chan = u_ref.shape[0]
    width = cols.size

    def taps(tap, side, add):
        @pl.loop(0, chan // BLOCK)
        def _(step):
            rows = pl.ds(pl.multiple_of(step * BLOCK, BLOCK), BLOCK)
            part = jnp.dot(w_ref[tap, rows, :], e_ref[side, :, cols], preferred_element_type=F32)
            dg_ref[rows, :] = dg_ref[rows, :] + part if add else part

    taps(1, 1, False)

    @pl.when(has_low)
    def _():
        taps(2, 0, True)

    @pl.when(has_up)
    def _():
        taps(0, 2, True)

    def inner_step(step, total):
        rows = pl.ds(pl.multiple_of(step * STRIP, STRIP), STRIP)
        dn = dg_ref[rows, :] * slope_ref[rows, cols]
        dg_ref[rows, :] = dn
        return total + jnp.sum(dn * u_ref[rows, cols].astype(F32), axis=0, keepdims=True)

    inner = lax.fori_loop(0, chan // STRIP, inner_step, jnp.zeros((1, width), F32)) / chan
    scale = scale_ref[:, cols]
    cubed = scale * scale * scale * inner

    @pl.loop(0, chan // STRIP)
    def _(step):
        rows = pl.ds(pl.multiple_of(step * STRIP, STRIP), STRIP)
        dinput = scale * dg_ref[rows, :] - u_ref[rows, cols].astype(F32) * cubed
        store(rows, (e_ref[1, rows, cols].astype(F32) + dinput).astype(BF16))


def kernel(
    count, spans, factor, reduce,
    h_ref, u1_ref, u2_ref, w1_hbm, w2_hbm, c1_ref, c2_ref,
    grad_ref, wgrad_ref,
    w1, w2, e, m, slope1, slope2, scale1, scale2, gelu1, dg, terms,
    w_sem, a_send, a_recv, b_send, b_recv, *more,
):
    span_first, span_second = spans
    z = lax.axis_index("seq")
    chan, width = u1_ref.shape
    share = h_ref.shape[0]
    piece = width // CHUNKS

    load2 = pltpu.make_async_copy(w2_hbm, w2, w_sem.at[0])
    load1 = pltpu.make_async_copy(w1_hbm, w1, w_sem.at[1])
    load2.start()
    load1.start()

    offsets = sorted(range(1, count), key=lambda j: -min(j, count - j))
    barrier = pltpu.get_barrier_semaphore()
    partners = [{"seq": lax.rem(z + j, count)} for j in offsets]
    if reduce:
        b = lax.axis_index("batch")
        x, core = b // 2, b % 2
        sib, across = x * 2 + 1 - core, (1 - x) * 2 + core
        partners += [{"batch": sib}, {"batch": across}]
    for partner in partners:
        pl.semaphore_signal(barrier, inc=1, device_id=partner, device_id_type=MESH)
    pl.semaphore_wait(barrier, len(partners))

    def valid(side, owner, span):
        if side == 0:
            return owner >= span
        return owner + span < count

    def share_copy(q, j, side, source, dest):
        shift = (side - 1) * span_second
        at = pl.multiple_of((dest + shift) * width, 128) + q * piece
        return pltpu.make_async_remote_copy(
            src_ref=h_ref.at[:, pl.ds(pl.multiple_of(at, 128), piece)],
            dst_ref=e.at[side, pl.ds(pl.multiple_of(source * share, 16), share), pl.ds(q * piece, piece)],
            send_sem=a_send.at[q, j - 1, side],
            recv_sem=a_recv.at[q, j - 1, side],
            device_id={"seq": dest},
            device_id_type=MESH,
        )

    def each_share(q, act, incoming):
        for j in offsets:
            source = lax.rem(z - j + count, count) if incoming else z
            dest = z if incoming else lax.rem(z + j, count)
            for side in (0, 1, 2):
                def go(side=side):
                    act(share_copy(q, j, side, source, dest))
                if side == 1:
                    go()
                else:
                    pl.when(valid(side, dest, span_second))(go)

    for q in range(CHUNKS):
        each_share(q, lambda copy: copy.start(), False)

    own = pl.ds(pl.multiple_of(z * share, 16), share)
    for side in (0, 1, 2):
        def keep(side=side):
            at = pl.multiple_of((z + (side - 1) * span_second) * width, 128)
            e[side, own, :] = h_ref[:, pl.ds(at, width)]
        if side == 1:
            keep()
        else:
            pl.when(valid(side, z, span_second))(keep)

    prepare(u2_ref, c2_ref, slope2, scale2, None)
    prepare(u1_ref, c1_ref, slope1, scale1, gelu1)
    load2.wait()

    def border_copy(q, side):
        to = z + span_first if side == 0 else z - span_first
        cols = pl.ds(q * piece, piece)
        return pltpu.make_async_remote_copy(
            src_ref=m.at[1, :, cols],
            dst_ref=m.at[side, :, cols],
            send_sem=b_send.at[q, side // 2],
            recv_sem=b_recv.at[q, side // 2],
            device_id={"seq": to},
            device_id_type=MESH,
        )

    sends_up = z + span_first < count
    sends_down = z >= span_first

    for q in range(CHUNKS):
        each_share(q, lambda copy: copy.wait_recv(), True)
        cols = pl.ds(q * piece, piece)

        def store_middle(rows, value):
            m[1, rows, cols] = value

        layer(
            w2, e, valid(0, z, span_second), valid(2, z, span_second), cols,
            u2_ref, slope2, scale2, dg, store_middle,
        )

        @pl.when(sends_up)
        def _():
            border_copy(q, 0).start()

        @pl.when(sends_down)
        def _():
            border_copy(q, 2).start()

    def tap_terms(tap, side):
        @pl.loop(0, chan // BLOCK)
        def _(step):
            start = pl.multiple_of(step * BLOCK, BLOCK)
            part = lax.dot_general(
                gelu1[pl.ds(start, BLOCK), :], m[side],
                (((1,), (1,)), ((), ())), preferred_element_type=F32,
            )
            terms[pl.ds(pl.multiple_of(tap * chan + start, BLOCK), BLOCK), :] = part * factor

    def border_terms(tap, side, has):
        @pl.when(has)
        def _():
            for q in range(CHUNKS):
                border_copy(q, side).wait_recv()
            tap_terms(tap, side)

        @pl.when(jnp.logical_not(has))
        def _():
            terms[pl.ds(tap * chan, chan), :] = jnp.zeros((chan, terms.shape[1]), F32)

    tap_terms(1, 1)
    border_terms(0, 2, sends_up)
    border_terms(2, 0, sends_down)
    load1.wait()

    def store_total(cols):
        def store(rows, value):
            grad_ref[rows, cols] = value
        return store

    def first_layer():
        for q in range(CHUNKS):
            cols = pl.ds(q * piece, piece)
            layer(
                w1, m, sends_down, sends_up, cols,
                u1_ref, slope1, scale1, dg, store_total(cols),
            )

    if reduce:
        reduce_terms(count, z, x, core, sib, across, terms, wgrad_ref, first_layer, *more)
    else:
        first_layer()
        wgrad_ref[...] = terms[...]

    for q in range(CHUNKS):
        each_share(q, lambda copy: copy.wait_send(), False)

        @pl.when(sends_up)
        def _():
            border_copy(q, 0).wait_send()

        @pl.when(sends_down)
        def _():
            border_copy(q, 2).wait_send()


def reduce_terms(
    count, z, x, core, sib, across, terms, wgrad_ref, meanwhile,
    core_out, core_in, x_out, x_in, z_out, z_in, kept, final,
    core_send, core_recv, x_send, x_recv, z_send, z_recv, f_send, f_recv,
):
    rows_each, half = core_out.shape[1:]
    order = sorted(range(count), key=lambda j: (j == 0, -min(j, count - j)))

    def rows_of(j, part):
        block = lax.rem(z + j, count)
        return pl.ds(pl.multiple_of(block * (2 * rows_each) + part * rows_each, 16), rows_each)

    mine = pl.ds(pl.multiple_of(core * half, 128), half)
    theirs = pl.ds(pl.multiple_of((1 - core) * half, 128), half)

    def core_copy(slot):
        return pltpu.make_async_remote_copy(
            src_ref=core_out.at[slot], dst_ref=core_in.at[slot],
            send_sem=core_send.at[slot], recv_sem=core_recv.at[slot],
            device_id={"batch": sib}, device_id_type=MESH,
        )

    def x_copy(j):
        return pltpu.make_async_remote_copy(
            src_ref=x_out.at[j], dst_ref=x_in.at[j],
            send_sem=x_send.at[j], recv_sem=x_recv.at[j],
            device_id={"batch": across}, device_id_type=MESH,
        )

    def z_copy(j, dest):
        return pltpu.make_async_remote_copy(
            src_ref=z_out.at[j - 1], dst_ref=z_in.at[j - 1],
            send_sem=z_send.at[j - 1], recv_sem=z_recv.at[j - 1],
            device_id={"seq": dest}, device_id_type=MESH,
        )

    for group, part in ((0, 1 - x), (1, x)):
        for j in order:
            slot = group * count + j
            core_out[slot] = terms[rows_of(j, part), theirs].astype(BF16)
            core_copy(slot).start()
    for j in order:
        core_copy(j).wait_recv()
        x_out[j] = (terms[rows_of(j, 1 - x), mine] + core_in[j].astype(F32)).astype(BF16)
        x_copy(j).start()

    meanwhile()

    for j in order:
        core_copy(count + j).wait_recv()
        x_copy(j).wait_recv()
        total = terms[rows_of(j, x), mine] + core_in[count + j].astype(F32) + x_in[j].astype(F32)
        if j == 0:
            kept[...] = total
        else:
            z_out[j - 1] = total.astype(BF16)
            z_copy(j, lax.rem(z + j, count)).start()
    for j in order[:-1]:
        z_copy(j, lax.rem(z + j, count)).wait_recv()
        kept[...] += z_in[j - 1].astype(F32)

    me = x * 2 + core
    final[me] = kept[...].astype(BF16)

    def final_copy(index, slot, to):
        return pltpu.make_async_remote_copy(
            src_ref=final.at[slot], dst_ref=final.at[slot],
            send_sem=f_send.at[index], recv_sem=f_recv.at[index],
            device_id={"batch": to}, device_id_type=MESH,
        )

    final_copy(0, me, across).start()
    final_copy(1, me, sib).start()
    final_copy(0, across, across).wait_recv()
    final_copy(2, across, sib).start()
    final_copy(1, sib, sib).wait_recv()
    final_copy(2, (1 - x) * 2 + 1 - core, sib).wait_recv()
    for part in range(2):
        for side in range(2):
            wgrad_ref[pl.ds(part * rows_each, rows_each), pl.ds(side * half, half)] = final[
                part * 2 + side
            ].astype(F32)

    final_copy(0, me, across).wait_send()
    final_copy(1, me, sib).wait_send()
    final_copy(2, across, sib).wait_send()
    for slot in range(2 * count):
        core_copy(slot).wait_send()
    for j in range(count):
        x_copy(j).wait_send()
    for j in range(1, count):
        z_copy(j, lax.rem(z + j, count)).wait_send()


def on_device(seq, batch, head, u1, u2, w1, w2, c1, c2):
    chan, width = u1.shape[1:]
    out_chan = w1.shape[2]
    taps = w1.shape[0]
    total_rows = taps * chan
    factor = 1.0 / math.sqrt(u1.shape[0] * batch * width * seq)
    spans = (DILATION_FIRST // width, DILATION_SECOND // width)
    rows = total_rows // seq
    reduce = batch == 4 and rows % 32 == 0 and out_chan % 256 == 0
    rows_each, half = rows // 2, out_chan // 2
    vmem = pl.BlockSpec(memory_space=pltpu.VMEM)
    anywhere = pl.BlockSpec(memory_space=pl.ANY)
    dma = pltpu.SemaphoreType.DMA
    scratch = [
        pltpu.VMEM(w1.shape, BF16),
        pltpu.VMEM(w2.shape, BF16),
        pltpu.VMEM((3, chan, width), BF16),
        pltpu.VMEM((3, chan, width), BF16),
        pltpu.VMEM((chan, width), F32),
        pltpu.VMEM((chan, width), F32),
        pltpu.VMEM((1, width), F32),
        pltpu.VMEM((1, width), F32),
        pltpu.VMEM((chan, width), BF16),
        pltpu.VMEM((chan, width // CHUNKS), F32),
        pltpu.VMEM((total_rows, out_chan), F32),
        dma((2,)),
        dma((CHUNKS, seq - 1, 3)),
        dma((CHUNKS, seq - 1, 3)),
        dma((CHUNKS, 2)),
        dma((CHUNKS, 2)),
    ]
    if reduce:
        scratch += [
            pltpu.VMEM((2 * seq, rows_each, half), BF16),
            pltpu.VMEM((2 * seq, rows_each, half), BF16),
            pltpu.VMEM((seq, rows_each, half), BF16),
            pltpu.VMEM((seq, rows_each, half), BF16),
            pltpu.VMEM((seq - 1, rows_each, half), BF16),
            pltpu.VMEM((seq - 1, rows_each, half), BF16),
            pltpu.VMEM((rows_each, half), F32),
            pltpu.VMEM((4, rows_each, half), BF16),
            dma((2 * seq,)),
            dma((2 * seq,)),
            dma((seq,)),
            dma((seq,)),
            dma((seq - 1,)),
            dma((seq - 1,)),
            dma((3,)),
            dma((3,)),
        ]
    grad, wgrad = pl.pallas_call(
        functools.partial(kernel, seq, spans, factor, reduce),
        out_shape=(
            jax.ShapeDtypeStruct((chan, width), BF16),
            jax.ShapeDtypeStruct((rows if reduce else total_rows, out_chan), F32),
        ),
        in_specs=[vmem, vmem, vmem, anywhere, anywhere, vmem, vmem],
        out_specs=(vmem, vmem),
        scratch_shapes=scratch,
        compiler_params=pltpu.CompilerParams(
            collective_id=0, has_side_effects=True, vmem_limit_bytes=56 * 1024 * 1024
        ),
        cost_estimate=pl.CostEstimate(
            flops=18 * chan * out_chan * width, bytes_accessed=20_000_000, transcendentals=2 * chan * width
        ),
    )(head[0], u1[0], u2[0], w1, w2, c1.reshape(chan, 1), c2.reshape(chan, 1))
    if not reduce:
        wgrad = lax.psum(lax.psum_scatter(wgrad, "seq", scatter_dimension=0, tiled=True), "batch")
    return grad[None], wgrad


def solution(mesh):
    in_specs = (
        P(("grp", "batch"), "seq", None),
        P(("grp", "batch"), None, "seq"),
        P(("grp", "batch"), None, "seq"),
        P(),
        P(),
        P(),
        P(),
    )
    out_specs = (P(("grp", "batch"), None, "seq"), P(("grp", "seq"), None))
    return jax.shard_map(
        functools.partial(on_device, mesh.shape["seq"], mesh.shape["batch"]),
        mesh=mesh, in_specs=in_specs, out_specs=out_specs, check_vma=False,
    )
```

```python
import functools
import math

import jax
import jax.numpy as jnp
from jax import lax
from jax.experimental import pallas as pl
from jax.experimental.pallas import tpu as pltpu
from jax.sharding import PartitionSpec as P

DILATION_FIRST = 512
DILATION_SECOND = 1024

EPS = 1e-06
SLOPE = math.sqrt(2.0 / math.pi)
CUBIC = 0.044715

F32 = jnp.float32
BF16 = jnp.bfloat16
MESH = pl.DeviceIdType.MESH
CHUNKS = 2
STRIP = 64
BLOCK = 256


def prepare(u_ref, gain_ref, slope_ref, scale_ref, gelu_ref):
    chan, width = u_ref.shape

    def square(step, total):
        rows = pl.ds(pl.multiple_of(step * STRIP, STRIP), STRIP)
        x = u_ref[rows, :].astype(F32)
        return total + jnp.sum(x * x, axis=0, keepdims=True)

    total = lax.fori_loop(0, chan // STRIP, square, jnp.zeros((1, width), F32))
    scale = lax.rsqrt(total / chan + EPS)
    scale_ref[...] = scale

    @pl.loop(0, chan // STRIP)
    def _(step):
        rows = pl.ds(pl.multiple_of(step * STRIP, STRIP), STRIP)
        gain = gain_ref[rows, 0:1]
        a = u_ref[rows, :].astype(F32) * scale * gain
        t = jnp.tanh(SLOPE * (a + CUBIC * a * a * a))
        slope = 0.5 * (1.0 + t) + 0.5 * a * (1.0 - t * t) * SLOPE * (1.0 + 3.0 * CUBIC * a * a)
        slope_ref[rows, :] = slope * gain
        if gelu_ref is not None:
            gelu_ref[rows, :] = (0.5 * a * (1.0 + t)).astype(BF16)


def layer(w_ref, e_ref, has_low, has_up, cols, u_ref, slope_ref, scale_ref, dg_ref, store):
    chan = u_ref.shape[0]
    width = cols.size

    def taps(tap, side, add):
        @pl.loop(0, chan // BLOCK)
        def _(step):
            rows = pl.ds(pl.multiple_of(step * BLOCK, BLOCK), BLOCK)
            part = jnp.dot(w_ref[tap, rows, :], e_ref[side, :, cols], preferred_element_type=F32)
            dg_ref[rows, :] = dg_ref[rows, :] + part if add else part

    taps(1, 1, False)

    @pl.when(has_low)
    def _():
        taps(2, 0, True)

    @pl.when(has_up)
    def _():
        taps(0, 2, True)

    def inner_step(step, total):
        rows = pl.ds(pl.multiple_of(step * STRIP, STRIP), STRIP)
        dn = dg_ref[rows, :] * slope_ref[rows, cols]
        dg_ref[rows, :] = dn
        return total + jnp.sum(dn * u_ref[rows, cols].astype(F32), axis=0, keepdims=True)

    inner = lax.fori_loop(0, chan // STRIP, inner_step, jnp.zeros((1, width), F32)) / chan
    scale = scale_ref[:, cols]
    cubed = scale * scale * scale * inner

    @pl.loop(0, chan // STRIP)
    def _(step):
        rows = pl.ds(pl.multiple_of(step * STRIP, STRIP), STRIP)
        dinput = scale * dg_ref[rows, :] - u_ref[rows, cols].astype(F32) * cubed
        store(rows, (e_ref[1, rows, cols].astype(F32) + dinput).astype(BF16))


def kernel(
    count, spans, factor, early,
    h_ref, u1_ref, u2_ref, w1_hbm, w2_hbm, c1_ref, c2_ref,
    grad_ref, wgrad_ref,
    gain1, gain2, w1, w2, e, m, slope1, slope2, scale1, scale2, gelu1, dg, terms,
    w_sem, a_send, a_recv, b_send, b_recv, *more,
):
    span_first, span_second = spans
    z = lax.axis_index("seq")
    chan, width = u1_ref.shape
    share = h_ref.shape[0]
    piece = width // CHUNKS

    load2 = pltpu.make_async_copy(w2_hbm, w2, w_sem.at[0])
    load1 = pltpu.make_async_copy(w1_hbm, w1, w_sem.at[1])
    load2.start()
    load1.start()

    offsets = sorted(range(1, count), key=lambda j: -min(j, count - j))
    barrier = pltpu.get_barrier_semaphore()
    partners = [{"seq": lax.rem(z + j, count)} for j in offsets]
    if early is not None:
        b = lax.axis_index("batch")
        x, core = b // 2, b % 2
        sib, across = x * 2 + 1 - core, (1 - x) * 2 + core
        partners += [{"batch": sib}, {"batch": across}]
    for partner in partners:
        pl.semaphore_signal(barrier, inc=1, device_id=partner, device_id_type=MESH)
    pl.semaphore_wait(barrier, len(partners))

    def valid(side, owner, span):
        if side == 0:
            return owner >= span
        return owner + span < count

    def share_copy(q, j, side, source, dest):
        shift = (side - 1) * span_second
        at = pl.multiple_of((dest + shift) * width, 128) + q * piece
        return pltpu.make_async_remote_copy(
            src_ref=h_ref.at[:, pl.ds(pl.multiple_of(at, 128), piece)],
            dst_ref=e.at[side, pl.ds(pl.multiple_of(source * share, 16), share), pl.ds(q * piece, piece)],
            send_sem=a_send.at[q, j - 1, side],
            recv_sem=a_recv.at[q, j - 1, side],
            device_id={"seq": dest},
            device_id_type=MESH,
        )

    def each_share(q, act, incoming):
        for j in offsets:
            source = lax.rem(z - j + count, count) if incoming else z
            dest = z if incoming else lax.rem(z + j, count)
            for side in (0, 1, 2):
                def go(side=side):
                    act(share_copy(q, j, side, source, dest))
                if side == 1:
                    go()
                else:
                    pl.when(valid(side, dest, span_second))(go)

    for q in range(CHUNKS):
        each_share(q, lambda copy: copy.start(), False)

    own = pl.ds(pl.multiple_of(z * share, 16), share)
    for side in (0, 1, 2):
        def keep(side=side):
            at = pl.multiple_of((z + (side - 1) * span_second) * width, 128)
            e[side, own, :] = h_ref[:, pl.ds(at, width)]
        if side == 1:
            keep()
        else:
            pl.when(valid(side, z, span_second))(keep)

    for gain, row in ((gain1, c1_ref), (gain2, c2_ref)):
        gain[...] = jnp.transpose(jnp.broadcast_to(row[...].reshape(1, chan), (gain.shape[1], chan)))
    prepare(u2_ref, gain2, slope2, scale2, None)
    prepare(u1_ref, gain1, slope1, scale1, gelu1)
    load2.wait()

    def border_copy(q, side):
        to = z + span_first if side == 0 else z - span_first
        cols = pl.ds(q * piece, piece)
        return pltpu.make_async_remote_copy(
            src_ref=m.at[1, :, cols],
            dst_ref=m.at[side, :, cols],
            send_sem=b_send.at[q, side // 2],
            recv_sem=b_recv.at[q, side // 2],
            device_id={"seq": to},
            device_id_type=MESH,
        )

    sends_up = z + span_first < count
    sends_down = z >= span_first

    for q in range(CHUNKS):
        each_share(q, lambda copy: copy.wait_recv(), True)
        cols = pl.ds(q * piece, piece)

        def store_middle(rows, value):
            m[1, rows, cols] = value

        layer(
            w2, e, valid(0, z, span_second), valid(2, z, span_second), cols,
            u2_ref, slope2, scale2, dg, store_middle,
        )

        @pl.when(sends_up)
        def _():
            border_copy(q, 0).start()

        @pl.when(sends_down)
        def _():
            border_copy(q, 2).start()

    def tap_terms(tap, side):
        @pl.loop(0, chan // BLOCK)
        def _(step):
            start = pl.multiple_of(step * BLOCK, BLOCK)
            part = lax.dot_general(
                gelu1[pl.ds(start, BLOCK), :], m[side],
                (((1,), (1,)), ((), ())), preferred_element_type=F32,
            )
            terms[pl.ds(pl.multiple_of(tap * chan + start, BLOCK), BLOCK), :] = part * factor

    def border_terms(tap, side, has):
        @pl.when(has)
        def _():
            for q in range(CHUNKS):
                border_copy(q, side).wait_recv()
            tap_terms(tap, side)

        @pl.when(jnp.logical_not(has))
        def _():
            terms[pl.ds(tap * chan, chan), :] = jnp.zeros((chan, terms.shape[1]), F32)

    tap_terms(1, 1)
    if early is not None:
        reduction = Reduction(z, x, core, sib, across, early, terms, more)
        reduction.start_early()
    border_terms(0, 2, sends_up)
    border_terms(2, 0, sends_down)
    load1.wait()

    def store_total(cols):
        def store(rows, value):
            grad_ref[rows, cols] = value
        return store

    def first_layer(q):
        cols = pl.ds(q * piece, piece)
        layer(
            w1, m, sends_down, sends_up, cols,
            u1_ref, slope1, scale1, dg, store_total(cols),
        )

    if early is not None:
        reduction.run(first_layer, wgrad_ref)
    else:
        for q in range(CHUNKS):
            first_layer(q)
        wgrad_ref[...] = terms[...]

    for q in range(CHUNKS):
        each_share(q, lambda copy: copy.wait_send(), False)

        @pl.when(sends_up)
        def _():
            border_copy(q, 0).wait_send()

        @pl.when(sends_down)
        def _():
            border_copy(q, 2).wait_send()


class Reduction:
    def __init__(self, z, x, core, sib, across, early, terms, refs):
        self.z, self.x, self.core, self.sib, self.across = z, x, core, sib, across
        self.terms = terms
        (self.core_out, self.core_in, self.x_out, self.x_in, self.z_out, self.z_in, self.kept,
         self.core_send, self.core_recv, self.x_send, self.x_recv,
         self.z_send, self.z_recv, self.f_send, self.f_recv) = refs
        self.each, self.half = self.core_out.shape[1:]
        self.mine = pl.ds(pl.multiple_of(core * self.half, 128), self.half)
        self.theirs = pl.ds(pl.multiple_of((1 - core) * self.half, 128), self.half)
        self.early_block = early[1] + x * (early[0] - early[1])
        self.early_unit = flip(self.early_block, z % 2, z // 2)

    def block(self, k):
        return flip(self.z, k % 2, k // 2)

    def rows(self, block, part):
        return pl.ds(pl.multiple_of((block * 2 + part) * self.each, 16), self.each)

    def core_copy(self, slot):
        return pltpu.make_async_remote_copy(
            src_ref=self.core_out.at[slot], dst_ref=self.core_in.at[slot],
            send_sem=self.core_send.at[slot], recv_sem=self.core_recv.at[slot],
            device_id={"batch": self.sib}, device_id_type=MESH,
        )

    def x_copy(self, k):
        return pltpu.make_async_remote_copy(
            src_ref=self.x_out.at[k], dst_ref=self.x_in.at[k],
            send_sem=self.x_send.at[k], recv_sem=self.x_recv.at[k],
            device_id={"batch": self.across}, device_id_type=MESH,
        )

    def z_copy(self, slot):
        return pltpu.make_async_remote_copy(
            src_ref=self.z_out.at[slot], dst_ref=self.z_in.at[slot],
            send_sem=self.z_send.at[slot], recv_sem=self.z_recv.at[slot],
            device_id={"seq": self.block(2 if slot == 2 else 1)}, device_id_type=MESH,
        )

    def to_core(self, slot, block, part):
        self.core_out[slot] = self.terms[self.rows(block, part), self.theirs].astype(BF16)
        self.core_copy(slot).start()

    def to_x(self, k, block):
        self.core_copy(k).wait_recv()
        own = self.terms[self.rows(block, 1 - self.x), self.mine]
        self.x_out[k] = (own + self.core_in[k].astype(F32)).astype(BF16)
        self.x_copy(k).start()

    def start_early(self):
        self.to_core(self.early_unit, self.early_block, 1 - self.x)
        self.to_x(self.early_unit, self.early_block)

    def run(self, meanwhile, final):
        for k in (3, 2, 1, 0):
            @pl.when(k != self.early_unit)
            def _():
                self.to_core(k, self.block(k), 1 - self.x)
        for k in (3, 2, 1, 0):
            self.to_core(4 + k, self.block(k), self.x)
        for k in (3, 2, 1, 0):
            @pl.when(k != self.early_unit)
            def _():
                self.to_x(k, self.block(k))
        meanwhile(0)
        for k in (3, 2, 1, 0):
            self.core_copy(4 + k).wait_recv()
            self.x_copy(k).wait_recv()
            own = self.terms[self.rows(self.block(k), self.x), self.mine]
            total = own + self.core_in[4 + k].astype(F32) + self.x_in[k].astype(F32)
            if k == 2:
                self.z_copy(0).wait_recv()
                total = total + self.z_in[0].astype(F32)
            if k == 0:
                self.kept[...] = total
            else:
                slot = {3: 0, 1: 1, 2: 2}[k]
                self.z_out[slot] = total.astype(BF16)
                self.z_copy(slot).start()
            if k == 3:
                meanwhile(1)
        self.z_copy(1).wait_recv()
        self.kept[...] += self.z_in[1].astype(F32)
        self.z_copy(2).wait_recv()
        me = self.x * 2 + self.core
        final[me] = (self.kept[...] + self.z_in[2].astype(F32)).astype(BF16)

        def final_copy(index, slot, to):
            return pltpu.make_async_remote_copy(
                src_ref=final.at[slot], dst_ref=final.at[slot],
                send_sem=self.f_send.at[index], recv_sem=self.f_recv.at[index],
                device_id={"batch": to}, device_id_type=MESH,
            )

        sib, across = self.sib, self.across
        final_copy(0, me, across).start()
        final_copy(1, me, sib).start()
        final_copy(0, across, across).wait_recv()
        final_copy(2, across, sib).start()
        final_copy(1, sib, sib).wait_recv()
        final_copy(2, (1 - self.x) * 2 + 1 - self.core, sib).wait_recv()

        final_copy(0, me, across).wait_send()
        final_copy(1, me, sib).wait_send()
        final_copy(2, across, sib).wait_send()
        for slot in range(8):
            self.core_copy(slot).wait_send()
        for k in range(4):
            self.x_copy(k).wait_send()
        for slot in range(3):
            self.z_copy(slot).wait_send()


def flip(value, bit, high):
    low_part, high_part = value % 2, value // 2
    return 2 * (high_part + high - 2 * high_part * high) + low_part + bit - 2 * low_part * bit


def finish(grad_hbm, parts_hbm, grad_out, wgrad_out, grad, parts, wgrad, sems):
    each, half = parts.shape[1:]
    into = pltpu.make_async_copy(grad_hbm, grad, sems.at[0])
    parts_in = pltpu.make_async_copy(parts_hbm, parts, sems.at[1])
    parts_in.start()
    into.start()
    parts_in.wait()
    out = []
    for part in range(2):
        rows = pl.ds(part * each, each)
        for side in range(2):
            wgrad[rows, pl.ds(side * half, half)] = parts[part * 2 + side].astype(F32)
        out.append(pltpu.make_async_copy(wgrad.at[rows], wgrad_out.at[rows], sems.at[3 + part]))
        out[-1].start()
    into.wait()
    out.append(pltpu.make_async_copy(grad, grad_out, sems.at[2]))
    out[-1].start()
    for copy in out:
        copy.wait()


def on_device(seq, batch, head, u1, u2, w1, w2, c1, c2):
    chan, width = u1.shape[1:]
    out_chan = w1.shape[2]
    taps = w1.shape[0]
    total_rows = taps * chan
    factor = 1.0 / math.sqrt(u1.shape[0] * batch * width * seq)
    spans = (DILATION_FIRST // width, DILATION_SECOND // width)
    rows = total_rows // seq
    rows_each, half = rows // 2, out_chan // 2
    early = [
        [
            block for block in range(seq)
            if chan <= (2 * block + part) * rows_each <= 2 * chan - rows_each
        ][:1]
        for part in range(2)
    ]
    reduce = (
        seq == 4 and batch == 4 and rows % 32 == 0 and out_chan % 256 == 0 and all(early)
    )
    early = [blocks[0] for blocks in early] if reduce else None
    vmem = pl.BlockSpec(memory_space=pltpu.VMEM)
    anywhere = pl.BlockSpec(memory_space=pl.ANY)
    dma = pltpu.SemaphoreType.DMA
    scratch = [
        pltpu.VMEM((chan, 128), F32),
        pltpu.VMEM((chan, 128), F32),
        pltpu.VMEM(w1.shape, BF16),
        pltpu.VMEM(w2.shape, BF16),
        pltpu.VMEM((3, chan, width), BF16),
        pltpu.VMEM((3, chan, width), BF16),
        pltpu.VMEM((chan, width), F32),
        pltpu.VMEM((chan, width), F32),
        pltpu.VMEM((1, width), F32),
        pltpu.VMEM((1, width), F32),
        pltpu.VMEM((chan, width), BF16),
        pltpu.VMEM((chan, width // CHUNKS), F32),
        pltpu.VMEM((total_rows, out_chan), F32),
        dma((2,)),
        dma((CHUNKS, seq - 1, 3)),
        dma((CHUNKS, seq - 1, 3)),
        dma((CHUNKS, 2)),
        dma((CHUNKS, 2)),
    ]
    if reduce:
        scratch += [
            pltpu.VMEM((2 * seq, rows_each, half), BF16),
            pltpu.VMEM((2 * seq, rows_each, half), BF16),
            pltpu.VMEM((seq, rows_each, half), BF16),
            pltpu.VMEM((seq, rows_each, half), BF16),
            pltpu.VMEM((seq - 1, rows_each, half), BF16),
            pltpu.VMEM((seq - 1, rows_each, half), BF16),
            pltpu.VMEM((rows_each, half), F32),
            dma((2 * seq,)),
            dma((2 * seq,)),
            dma((seq,)),
            dma((seq,)),
            dma((seq - 1,)),
            dma((seq - 1,)),
            dma((3,)),
            dma((3,)),
        ]
    grad, wgrad = pl.pallas_call(
        functools.partial(kernel, seq, spans, factor, early),
        out_shape=(
            jax.ShapeDtypeStruct((chan, width), BF16),
            jax.ShapeDtypeStruct((4, rows_each, half), BF16)
            if reduce else jax.ShapeDtypeStruct((total_rows, out_chan), F32),
        ),
        in_specs=[vmem, vmem, vmem, anywhere, anywhere, vmem, vmem],
        out_specs=(vmem, vmem),
        scratch_shapes=scratch,
        compiler_params=pltpu.CompilerParams(
            collective_id=0, has_side_effects=True, vmem_limit_bytes=56 * 1024 * 1024
        ),
        cost_estimate=pl.CostEstimate(
            flops=18 * chan * out_chan * width, bytes_accessed=20_000_000, transcendentals=2 * chan * width
        ),
    )(head[0], u1[0], u2[0], w1, w2, c1, c2)
    if reduce:
        shapes = (
            jax.ShapeDtypeStruct(grad.shape, BF16),
            jax.ShapeDtypeStruct((rows, out_chan), F32),
        )
        grad, wgrad = pl.pallas_call(
            finish,
            out_shape=shapes,
            in_specs=[anywhere, anywhere],
            out_specs=(anywhere, anywhere),
            scratch_shapes=[
                pltpu.VMEM(grad.shape, BF16),
                pltpu.VMEM(wgrad.shape, BF16),
                pltpu.VMEM((rows, out_chan), F32),
                dma((5,)),
            ],
            compiler_params=pltpu.CompilerParams(vmem_limit_bytes=56 * 1024 * 1024),
        )(grad, wgrad)
    else:
        wgrad = lax.psum(lax.psum_scatter(wgrad, "seq", scatter_dimension=0, tiled=True), "batch")
    return grad[None], wgrad


def solution(mesh):
    in_specs = (
        P(("grp", "batch"), "seq", None),
        P(("grp", "batch"), None, "seq"),
        P(("grp", "batch"), None, "seq"),
        P(),
        P(),
        P(),
        P(),
    )
    out_specs = (P(("grp", "batch"), None, "seq"), P(("grp", "seq"), None))
    return jax.shard_map(
        functools.partial(on_device, mesh.shape["seq"], mesh.shape["batch"]),
        mesh=mesh, in_specs=in_specs, out_specs=out_specs, check_vma=False,
    )
```

```python
import functools
import math

import jax
import jax.numpy as jnp
from jax import lax
from jax.experimental import pallas as pl
from jax.experimental.pallas import tpu as pltpu
from jax.sharding import PartitionSpec as P

DILATION_FIRST = 512
DILATION_SECOND = 1024

EPS = 1e-06
SLOPE = math.sqrt(2.0 / math.pi)
CUBIC = 0.044715

F32 = jnp.float32
BF16 = jnp.bfloat16
MESH = pl.DeviceIdType.MESH
CHUNKS = 2
STRIP = 64
BLOCK = 768


def prepare(u_ref, gain_ref, slope_ref, scale_ref, gelu_ref):
    chan, width = u_ref.shape

    def square(step, total):
        rows = pl.ds(pl.multiple_of(step * STRIP, STRIP), STRIP)
        x = u_ref[rows, :].astype(F32)
        return total + jnp.sum(x * x, axis=0, keepdims=True)

    total = lax.fori_loop(0, chan // STRIP, square, jnp.zeros((1, width), F32))
    scale = lax.rsqrt(total / chan + EPS)
    scale_ref[...] = scale

    @pl.loop(0, chan // STRIP)
    def _(step):
        rows = pl.ds(pl.multiple_of(step * STRIP, STRIP), STRIP)
        gain = gain_ref[rows, 0:1]
        a = u_ref[rows, :].astype(F32) * scale * gain
        t = jnp.tanh(SLOPE * (a + CUBIC * a * a * a))
        slope = 0.5 * (1.0 + t) + 0.5 * a * (1.0 - t * t) * SLOPE * (1.0 + 3.0 * CUBIC * a * a)
        slope_ref[rows, :] = slope * gain
        if gelu_ref is not None:
            gelu_ref[rows, :] = (0.5 * a * (1.0 + t)).astype(BF16)


def layer(w_ref, e_ref, has_low, has_up, cols, u_ref, slope_ref, scale_ref, dg_ref, store):
    chan = u_ref.shape[0]
    width = cols.size

    def taps(tap, side, add):
        @pl.loop(0, chan // BLOCK)
        def _(step):
            rows = pl.ds(pl.multiple_of(step * BLOCK, BLOCK), BLOCK)
            part = jnp.dot(w_ref[tap, rows, :], e_ref[side, :, cols], preferred_element_type=F32)
            dg_ref[rows, :] = dg_ref[rows, :] + part if add else part

    taps(1, 1, False)

    @pl.when(has_low)
    def _():
        taps(2, 0, True)

    @pl.when(has_up)
    def _():
        taps(0, 2, True)

    def inner_step(step, total):
        rows = pl.ds(pl.multiple_of(step * STRIP, STRIP), STRIP)
        dn = dg_ref[rows, :] * slope_ref[rows, cols]
        dg_ref[rows, :] = dn
        return total + jnp.sum(dn * u_ref[rows, cols].astype(F32), axis=0, keepdims=True)

    inner = lax.fori_loop(0, chan // STRIP, inner_step, jnp.zeros((1, width), F32)) / chan
    scale = scale_ref[:, cols]
    cubed = scale * scale * scale * inner

    @pl.loop(0, chan // STRIP)
    def _(step):
        rows = pl.ds(pl.multiple_of(step * STRIP, STRIP), STRIP)
        dinput = scale * dg_ref[rows, :] - u_ref[rows, cols].astype(F32) * cubed
        store(rows, (e_ref[1, rows, cols].astype(F32) + dinput).astype(BF16))


def kernel(
    count, spans, factor, early,
    h_ref, u1_hbm, u2_hbm, w1_hbm, w2_hbm, c1_ref, c2_ref,
    grad_hbm, wgrad_hbm,
    u1_ref, u2_ref, grad_ref, gain1, gain2, w1, w2, e, m, slope1, slope2, scale1, scale2, gelu1, dg, terms,
    w_sem, a_send, a_recv, b_send, b_recv, *more,
):
    span_first, span_second = spans
    z = lax.axis_index("seq")
    chan, width = u1_ref.shape
    share = h_ref.shape[0]
    piece = width // CHUNKS

    load2 = pltpu.make_async_copy(w2_hbm, w2, w_sem.at[0])
    load1 = pltpu.make_async_copy(w1_hbm, w1, w_sem.at[1])
    load_u2 = pltpu.make_async_copy(u2_hbm, u2_ref, w_sem.at[2])
    load_u1 = pltpu.make_async_copy(u1_hbm, u1_ref, w_sem.at[3])

    offsets = sorted(range(1, count), key=lambda j: -min(j, count - j))
    barrier = pltpu.get_barrier_semaphore()
    partners = [{"seq": lax.rem(z + j, count)} for j in offsets]
    if early is not None:
        b = lax.axis_index("batch")
        x, core = b // 2, b % 2
        sib, across = x * 2 + 1 - core, (1 - x) * 2 + core
        partners += [{"batch": sib}, {"batch": across}]
    for partner in partners:
        pl.semaphore_signal(barrier, inc=1, device_id=partner, device_id_type=MESH)
    pl.semaphore_wait(barrier, len(partners))

    def valid(side, owner, span):
        if side == 0:
            return owner >= span
        return owner + span < count

    def share_copy(q, j, side, source, dest):
        shift = (side - 1) * span_second
        at = pl.multiple_of((dest + shift) * width, 128) + q * piece
        return pltpu.make_async_remote_copy(
            src_ref=h_ref.at[:, pl.ds(pl.multiple_of(at, 128), piece)],
            dst_ref=e.at[side, pl.ds(pl.multiple_of(source * share, 16), share), pl.ds(q * piece, piece)],
            send_sem=a_send.at[q, j - 1, side],
            recv_sem=a_recv.at[q, j - 1, side],
            device_id={"seq": dest},
            device_id_type=MESH,
        )

    def each_share(q, act, incoming):
        for j in offsets:
            source = lax.rem(z - j + count, count) if incoming else z
            dest = z if incoming else lax.rem(z + j, count)
            for side in (0, 1, 2):
                def go(side=side):
                    act(share_copy(q, j, side, source, dest))
                if side == 1:
                    go()
                else:
                    pl.when(valid(side, dest, span_second))(go)

    for q in range(CHUNKS):
        each_share(q, lambda copy: copy.start(), False)

    own = pl.ds(pl.multiple_of(z * share, 16), share)

    def each_own(act):
        for side in (0, 1, 2):
            def keep(side=side):
                at = pl.multiple_of((z + (side - 1) * span_second) * width, 128)
                act(pltpu.make_async_copy(
                    h_ref.at[:, pl.ds(at, width)], e.at[side, own, :], w_sem.at[4 + side]
                ))
            if side == 1:
                keep()
            else:
                pl.when(valid(side, z, span_second))(keep)

    load_u2.start()
    load_u1.start()
    each_own(lambda copy: copy.start())
    load2.start()
    load1.start()
    for gain, row in ((gain1, c1_ref), (gain2, c2_ref)):
        gain[...] = jnp.transpose(jnp.broadcast_to(row[...].reshape(1, chan), (gain.shape[1], chan)))
    load_u2.wait()
    prepare(u2_ref, gain2, slope2, scale2, None)
    load_u1.wait()
    prepare(u1_ref, gain1, slope1, scale1, gelu1)
    load2.wait()
    each_own(lambda copy: copy.wait())

    def border_copy(q, side):
        to = z + span_first if side == 0 else z - span_first
        cols = pl.ds(q * piece, piece)
        return pltpu.make_async_remote_copy(
            src_ref=m.at[1, :, cols],
            dst_ref=m.at[side, :, cols],
            send_sem=b_send.at[q, side // 2],
            recv_sem=b_recv.at[q, side // 2],
            device_id={"seq": to},
            device_id_type=MESH,
        )

    sends_up = z + span_first < count
    sends_down = z >= span_first

    for q in range(CHUNKS):
        each_share(q, lambda copy: copy.wait_recv(), True)
        cols = pl.ds(q * piece, piece)

        def store_middle(rows, value):
            m[1, rows, cols] = value

        layer(
            w2, e, valid(0, z, span_second), valid(2, z, span_second), cols,
            u2_ref, slope2, scale2, dg, store_middle,
        )

        @pl.when(sends_up)
        def _():
            border_copy(q, 0).start()

        @pl.when(sends_down)
        def _():
            border_copy(q, 2).start()

    def tap_terms(tap, side):
        @pl.loop(0, chan // BLOCK)
        def _(step):
            start = pl.multiple_of(step * BLOCK, BLOCK)
            part = lax.dot_general(
                gelu1[pl.ds(start, BLOCK), :], m[side],
                (((1,), (1,)), ((), ())), preferred_element_type=F32,
            )
            terms[pl.ds(pl.multiple_of(tap * chan + start, BLOCK), BLOCK), :] = part * factor

    def border_terms(tap, side, has):
        @pl.when(has)
        def _():
            for q in range(CHUNKS):
                border_copy(q, side).wait_recv()
            tap_terms(tap, side)

        @pl.when(jnp.logical_not(has))
        def _():
            terms[pl.ds(tap * chan, chan), :] = jnp.zeros((chan, terms.shape[1]), F32)

    tap_terms(1, 1)
    if early is not None:
        reduction = Reduction(z, x, core, sib, across, early, terms, more)
        reduction.start_early()
    border_terms(0, 2, sends_up)
    border_terms(2, 0, sends_down)
    load1.wait()

    def store_total(cols):
        def store(rows, value):
            grad_ref[rows, cols] = value
        return store

    def result_copy(q):
        cols = pl.ds(q * piece, piece)
        return pltpu.make_async_copy(grad_ref.at[:, cols], grad_hbm.at[:, cols], w_sem.at[7 + q])

    def first_layer(q):
        cols = pl.ds(q * piece, piece)
        layer(
            w1, m, sends_down, sends_up, cols,
            u1_ref, slope1, scale1, dg, store_total(cols),
        )
        result_copy(q).start()

    if early is not None:
        reduction.run(first_layer, wgrad_hbm)
    else:
        for q in range(CHUNKS):
            first_layer(q)
        terms_out = pltpu.make_async_copy(terms, wgrad_hbm, w_sem.at[0])
        terms_out.start()
        terms_out.wait()
    for q in range(CHUNKS):
        result_copy(q).wait()

    for q in range(CHUNKS):
        each_share(q, lambda copy: copy.wait_send(), False)

        @pl.when(sends_up)
        def _():
            border_copy(q, 0).wait_send()

        @pl.when(sends_down)
        def _():
            border_copy(q, 2).wait_send()


class Reduction:
    def __init__(self, z, x, core, sib, across, early, terms, refs):
        self.z, self.x, self.core, self.sib, self.across = z, x, core, sib, across
        self.terms = terms
        (self.core_out, self.core_in, self.x_out, self.x_in, self.z_out, self.z_in, self.kept, self.final,
         self.core_send, self.core_recv, self.x_send, self.x_recv,
         self.z_send, self.z_recv, self.f_send, self.f_recv, self.o_sem) = refs
        self.each, self.half = self.core_out.shape[1:]
        self.mine = pl.ds(pl.multiple_of(core * self.half, 128), self.half)
        self.theirs = pl.ds(pl.multiple_of((1 - core) * self.half, 128), self.half)
        self.early_block = early[1] + x * (early[0] - early[1])
        self.early_unit = flip(self.early_block, z % 2, z // 2)

    def block(self, k):
        return flip(self.z, k % 2, k // 2)

    def rows(self, block, part):
        return pl.ds(pl.multiple_of((block * 2 + part) * self.each, 16), self.each)

    def core_copy(self, slot):
        return pltpu.make_async_remote_copy(
            src_ref=self.core_out.at[slot], dst_ref=self.core_in.at[slot],
            send_sem=self.core_send.at[slot], recv_sem=self.core_recv.at[slot],
            device_id={"batch": self.sib}, device_id_type=MESH,
        )

    def x_copy(self, k):
        return pltpu.make_async_remote_copy(
            src_ref=self.x_out.at[k], dst_ref=self.x_in.at[k],
            send_sem=self.x_send.at[k], recv_sem=self.x_recv.at[k],
            device_id={"batch": self.across}, device_id_type=MESH,
        )

    def z_copy(self, slot):
        return pltpu.make_async_remote_copy(
            src_ref=self.z_out.at[slot], dst_ref=self.z_in.at[slot],
            send_sem=self.z_send.at[slot], recv_sem=self.z_recv.at[slot],
            device_id={"seq": self.block(2 if slot == 2 else 1)}, device_id_type=MESH,
        )

    def to_core(self, slot, block, part):
        self.core_out[slot] = self.terms[self.rows(block, part), self.theirs].astype(BF16)
        self.core_copy(slot).start()

    def to_x(self, k, block):
        self.core_copy(k).wait_recv()
        own = self.terms[self.rows(block, 1 - self.x), self.mine]
        self.x_out[k] = (own + self.core_in[k].astype(F32)).astype(BF16)
        self.x_copy(k).start()

    def start_early(self):
        self.to_core(self.early_unit, self.early_block, 1 - self.x)
        self.to_x(self.early_unit, self.early_block)

    def run(self, meanwhile, wgrad_hbm):
        final = self.final
        for k in (3, 2, 1, 0):
            @pl.when(k != self.early_unit)
            def _():
                self.to_core(k, self.block(k), 1 - self.x)
        for k in (3, 2, 1, 0):
            self.to_core(4 + k, self.block(k), self.x)
        for k in (3, 2, 1, 0):
            @pl.when(k != self.early_unit)
            def _():
                self.to_x(k, self.block(k))
        meanwhile(0)
        for k in (3, 2, 1, 0):
            self.core_copy(4 + k).wait_recv()
            self.x_copy(k).wait_recv()
            own = self.terms[self.rows(self.block(k), self.x), self.mine]
            total = own + self.core_in[4 + k].astype(F32) + self.x_in[k].astype(F32)
            if k == 2:
                self.z_copy(0).wait_recv()
                total = total + self.z_in[0].astype(F32)
            if k == 0:
                self.kept[...] = total
            else:
                slot = {3: 0, 1: 1, 2: 2}[k]
                self.z_out[slot] = total.astype(BF16)
                self.z_copy(slot).start()
            if k == 3:
                meanwhile(1)
        self.z_copy(1).wait_recv()
        self.kept[...] += self.z_in[1].astype(F32)
        self.z_copy(2).wait_recv()
        me = self.x * 2 + self.core
        final[me] = (self.kept[...] + self.z_in[2].astype(F32)).astype(BF16)

        def final_copy(index, slot, to):
            return pltpu.make_async_remote_copy(
                src_ref=final.at[slot], dst_ref=final.at[slot],
                send_sem=self.f_send.at[index], recv_sem=self.f_recv.at[index],
                device_id={"batch": to}, device_id_type=MESH,
            )

        sib, across = self.sib, self.across
        final_copy(0, me, across).start()
        final_copy(1, me, sib).start()
        last = (1 - self.x) * 2 + 1 - self.core

        def out_copy(slot):
            return pltpu.make_async_copy(final.at[slot], wgrad_hbm.at[slot], self.o_sem.at[slot])

        out_copy(me).start()
        final_copy(1, sib, sib).wait_recv()
        out_copy(sib).start()
        final_copy(0, across, across).wait_recv()
        final_copy(2, across, sib).start()
        out_copy(across).start()
        final_copy(2, last, sib).wait_recv()
        out_copy(last).start()

        final_copy(0, me, across).wait_send()
        final_copy(1, me, sib).wait_send()
        final_copy(2, across, sib).wait_send()
        for slot in range(8):
            self.core_copy(slot).wait_send()
        for k in range(4):
            self.x_copy(k).wait_send()
        for slot in range(3):
            self.z_copy(slot).wait_send()
        for slot in range(4):
            out_copy(slot).wait()


def flip(value, bit, high):
    low_part, high_part = value % 2, value // 2
    return 2 * (high_part + high - 2 * high_part * high) + low_part + bit - 2 * low_part * bit


def finish(grad_hbm, parts_hbm, grad_out, wgrad_out, grad, parts, wgrad, sems):
    each, half = parts.shape[1:]
    into = pltpu.make_async_copy(grad_hbm, grad, sems.at[0])
    parts_in = pltpu.make_async_copy(parts_hbm, parts, sems.at[1])
    parts_in.start()
    into.start()
    parts_in.wait()
    out = []
    for part in range(2):
        rows = pl.ds(part * each, each)
        for side in range(2):
            wgrad[rows, pl.ds(side * half, half)] = parts[part * 2 + side].astype(F32)
        out.append(pltpu.make_async_copy(wgrad.at[rows], wgrad_out.at[rows], sems.at[3 + part]))
        out[-1].start()
    into.wait()
    out.append(pltpu.make_async_copy(grad, grad_out, sems.at[2]))
    out[-1].start()
    for copy in out:
        copy.wait()


def on_device(seq, batch, head, u1, u2, w1, w2, c1, c2):
    chan, width = u1.shape[1:]
    out_chan = w1.shape[2]
    taps = w1.shape[0]
    total_rows = taps * chan
    factor = 1.0 / math.sqrt(u1.shape[0] * batch * width * seq)
    spans = (DILATION_FIRST // width, DILATION_SECOND // width)
    rows = total_rows // seq
    rows_each, half = rows // 2, out_chan // 2
    early = [
        [
            block for block in range(seq)
            if chan <= (2 * block + part) * rows_each <= 2 * chan - rows_each
        ][:1]
        for part in range(2)
    ]
    reduce = (
        seq == 4 and batch == 4 and rows % 32 == 0 and out_chan % 256 == 0 and all(early)
    )
    early = [blocks[0] for blocks in early] if reduce else None
    vmem = pl.BlockSpec(memory_space=pltpu.VMEM)
    anywhere = pl.BlockSpec(memory_space=pl.ANY)
    dma = pltpu.SemaphoreType.DMA
    scratch = [
        pltpu.VMEM((chan, width), BF16),
        pltpu.VMEM((chan, width), BF16),
        pltpu.VMEM((chan, width), BF16),
        pltpu.VMEM((chan, 128), F32),
        pltpu.VMEM((chan, 128), F32),
        pltpu.VMEM(w1.shape, BF16),
        pltpu.VMEM(w2.shape, BF16),
        pltpu.VMEM((3, chan, width), BF16),
        pltpu.VMEM((3, chan, width), BF16),
        pltpu.VMEM((chan, width), F32),
        pltpu.VMEM((chan, width), F32),
        pltpu.VMEM((1, width), F32),
        pltpu.VMEM((1, width), F32),
        pltpu.VMEM((chan, width), BF16),
        pltpu.VMEM((chan, width // CHUNKS), F32),
        pltpu.VMEM((total_rows, out_chan), F32),
        dma((7 + CHUNKS,)),
        dma((CHUNKS, seq - 1, 3)),
        dma((CHUNKS, seq - 1, 3)),
        dma((CHUNKS, 2)),
        dma((CHUNKS, 2)),
    ]
    if reduce:
        scratch += [
            pltpu.VMEM((2 * seq, rows_each, half), BF16),
            pltpu.VMEM((2 * seq, rows_each, half), BF16),
            pltpu.VMEM((seq, rows_each, half), BF16),
            pltpu.VMEM((seq, rows_each, half), BF16),
            pltpu.VMEM((seq - 1, rows_each, half), BF16),
            pltpu.VMEM((seq - 1, rows_each, half), BF16),
            pltpu.VMEM((rows_each, half), F32),
            pltpu.VMEM((4, rows_each, half), BF16),
            dma((2 * seq,)),
            dma((2 * seq,)),
            dma((seq,)),
            dma((seq,)),
            dma((seq - 1,)),
            dma((seq - 1,)),
            dma((3,)),
            dma((3,)),
            dma((4,)),
        ]
    grad, wgrad = pl.pallas_call(
        functools.partial(kernel, seq, spans, factor, early),
        out_shape=(
            jax.ShapeDtypeStruct((chan, width), BF16),
            jax.ShapeDtypeStruct((4, rows_each, half), BF16)
            if reduce else jax.ShapeDtypeStruct((total_rows, out_chan), F32),
        ),
        in_specs=[anywhere] * 5 + [vmem, vmem],
        out_specs=(anywhere, anywhere),
        scratch_shapes=scratch,
        compiler_params=pltpu.CompilerParams(
            collective_id=0, has_side_effects=True, vmem_limit_bytes=56 * 1024 * 1024
        ),
        cost_estimate=pl.CostEstimate(
            flops=18 * chan * out_chan * width, bytes_accessed=20_000_000, transcendentals=2 * chan * width
        ),
    )(head[0], u1[0], u2[0], w1, w2, c1, c2)
    if reduce:
        shapes = (
            jax.ShapeDtypeStruct(grad.shape, BF16),
            jax.ShapeDtypeStruct((rows, out_chan), F32),
        )
        grad, wgrad = pl.pallas_call(
            finish,
            out_shape=shapes,
            in_specs=[anywhere, anywhere],
            out_specs=(anywhere, anywhere),
            scratch_shapes=[
                pltpu.VMEM(grad.shape, BF16),
                pltpu.VMEM(wgrad.shape, BF16),
                pltpu.VMEM((rows, out_chan), F32),
                dma((5,)),
            ],
            compiler_params=pltpu.CompilerParams(vmem_limit_bytes=56 * 1024 * 1024),
        )(grad, wgrad)
    else:
        wgrad = lax.psum(lax.psum_scatter(wgrad, "seq", scatter_dimension=0, tiled=True), "batch")
    return grad[None], wgrad


def solution(mesh):
    in_specs = (
        P(("grp", "batch"), "seq", None),
        P(("grp", "batch"), None, "seq"),
        P(("grp", "batch"), None, "seq"),
        P(),
        P(),
        P(),
        P(),
    )
    out_specs = (P(("grp", "batch"), None, "seq"), P(("grp", "seq"), None))
    return jax.shard_map(
        functools.partial(on_device, mesh.shape["seq"], mesh.shape["batch"]),
        mesh=mesh, in_specs=in_specs, out_specs=out_specs, check_vma=False,
    )
```

```python
import functools
import math

import jax
import jax.numpy as jnp
from jax import lax
from jax.experimental import pallas as pl
from jax.experimental.pallas import tpu as pltpu
from jax.sharding import PartitionSpec as P

DILATION_FIRST = 512
DILATION_SECOND = 1024

EPS = 1e-06
SLOPE = math.sqrt(2.0 / math.pi)
CUBIC = 0.044715

F32 = jnp.float32
BF16 = jnp.bfloat16
MESH = pl.DeviceIdType.MESH
CHUNKS = 4
STRIP = 64
BLOCK = 768


def prepare(u_ref, gain_ref, slope_ref, scale_ref, gelu_ref):
    chan, width = u_ref.shape

    def square(step, total):
        rows = pl.ds(pl.multiple_of(step * STRIP, STRIP), STRIP)
        x = u_ref[rows, :].astype(F32)
        return total + jnp.sum(x * x, axis=0, keepdims=True)

    total = lax.fori_loop(0, chan // STRIP, square, jnp.zeros((1, width), F32))
    scale = lax.rsqrt(total / chan + EPS)
    scale_ref[...] = scale

    @pl.loop(0, chan // STRIP)
    def _(step):
        rows = pl.ds(pl.multiple_of(step * STRIP, STRIP), STRIP)
        gain = gain_ref[rows, 0:1]
        a = u_ref[rows, :].astype(F32) * scale * gain
        t = jnp.tanh(SLOPE * (a + CUBIC * a * a * a))
        slope = 0.5 * (1.0 + t) + 0.5 * a * (1.0 - t * t) * SLOPE * (1.0 + 3.0 * CUBIC * a * a)
        slope_ref[rows, :] = slope * gain
        if gelu_ref is not None:
            gelu_ref[rows, :] = (0.5 * a * (1.0 + t)).astype(BF16)


def layer(w_ref, e_ref, has_low, has_up, cols, u_ref, slope_ref, scale_ref, dg_ref, store):
    chan = u_ref.shape[0]
    width = cols.size

    def taps(tap, side, add):
        @pl.loop(0, chan // BLOCK)
        def _(step):
            rows = pl.ds(pl.multiple_of(step * BLOCK, BLOCK), BLOCK)
            part = jnp.dot(w_ref[tap, rows, :], e_ref[side, :, cols], preferred_element_type=F32)
            dg_ref[rows, :] = dg_ref[rows, :] + part if add else part

    taps(1, 1, False)

    @pl.when(has_low)
    def _():
        taps(2, 0, True)

    @pl.when(has_up)
    def _():
        taps(0, 2, True)

    def inner_step(step, total):
        rows = pl.ds(pl.multiple_of(step * STRIP, STRIP), STRIP)
        dn = dg_ref[rows, :] * slope_ref[rows, cols]
        dg_ref[rows, :] = dn
        return total + jnp.sum(dn * u_ref[rows, cols].astype(F32), axis=0, keepdims=True)

    inner = lax.fori_loop(0, chan // STRIP, inner_step, jnp.zeros((1, width), F32)) / chan
    scale = scale_ref[:, cols]
    cubed = scale * scale * scale * inner

    @pl.loop(0, chan // STRIP)
    def _(step):
        rows = pl.ds(pl.multiple_of(step * STRIP, STRIP), STRIP)
        dinput = scale * dg_ref[rows, :] - u_ref[rows, cols].astype(F32) * cubed
        store(rows, (e_ref[1, rows, cols].astype(F32) + dinput).astype(BF16))


def kernel(
    count, spans, factor, early,
    h_ref, u1_hbm, u2_hbm, w1_hbm, w2_hbm, c1_ref, c2_ref,
    grad_hbm, wgrad_hbm,
    u1_ref, u2_ref, grad_ref, gain1, gain2, w1, w2, e, m, slope1, slope2, scale1, scale2, gelu1, dg, terms,
    w_sem, a_send, a_recv, b_send, b_recv, *more,
):
    span_first, span_second = spans
    z = lax.axis_index("seq")
    chan, width = u1_ref.shape
    share = h_ref.shape[0]
    piece = width // CHUNKS

    load2 = pltpu.make_async_copy(w2_hbm, w2, w_sem.at[0])
    load1 = pltpu.make_async_copy(w1_hbm, w1, w_sem.at[1])
    load_u2 = pltpu.make_async_copy(u2_hbm, u2_ref, w_sem.at[2])
    load_u1 = pltpu.make_async_copy(u1_hbm, u1_ref, w_sem.at[3])

    offsets = sorted(range(1, count), key=lambda j: -min(j, count - j))
    barrier = pltpu.get_barrier_semaphore()
    partners = [{"seq": lax.rem(z + j, count)} for j in offsets]
    if early is not None:
        b = lax.axis_index("batch")
        x, core = b // 2, b % 2
        sib, across = x * 2 + 1 - core, (1 - x) * 2 + core
        partners += [{"batch": sib}, {"batch": across}]
    for partner in partners:
        pl.semaphore_signal(barrier, inc=1, device_id=partner, device_id_type=MESH)
    pl.semaphore_wait(barrier, len(partners))

    def valid(side, owner, span):
        if side == 0:
            return owner >= span
        return owner + span < count

    def share_copy(q, j, side, source, dest):
        shift = (side - 1) * span_second
        at = pl.multiple_of((dest + shift) * width, 128) + q * piece
        return pltpu.make_async_remote_copy(
            src_ref=h_ref.at[:, pl.ds(pl.multiple_of(at, 128), piece)],
            dst_ref=e.at[side, pl.ds(pl.multiple_of(source * share, 16), share), pl.ds(q * piece, piece)],
            send_sem=a_send.at[q, j - 1, side],
            recv_sem=a_recv.at[q, j - 1, side],
            device_id={"seq": dest},
            device_id_type=MESH,
        )

    def each_share(q, act, incoming):
        for j in offsets:
            source = lax.rem(z - j + count, count) if incoming else z
            dest = z if incoming else lax.rem(z + j, count)
            for side in (0, 1, 2):
                def go(side=side):
                    act(share_copy(q, j, side, source, dest))
                if side == 1:
                    go()
                else:
                    pl.when(valid(side, dest, span_second))(go)

    for q in range(CHUNKS):
        each_share(q, lambda copy: copy.start(), False)

    own = pl.ds(pl.multiple_of(z * share, 16), share)

    def each_own(act):
        for side in (0, 1, 2):
            def keep(side=side):
                at = pl.multiple_of((z + (side - 1) * span_second) * width, 128)
                act(pltpu.make_async_copy(
                    h_ref.at[:, pl.ds(at, width)], e.at[side, own, :], w_sem.at[4 + side]
                ))
            if side == 1:
                keep()
            else:
                pl.when(valid(side, z, span_second))(keep)

    load_u2.start()
    load_u1.start()
    each_own(lambda copy: copy.start())
    load2.start()
    load1.start()
    for gain, row in ((gain1, c1_ref), (gain2, c2_ref)):
        gain[...] = jnp.transpose(jnp.broadcast_to(row[...].reshape(1, chan), (gain.shape[1], chan)))
    load_u2.wait()
    prepare(u2_ref, gain2, slope2, scale2, None)
    load_u1.wait()
    prepare(u1_ref, gain1, slope1, scale1, gelu1)
    load2.wait()
    each_own(lambda copy: copy.wait())

    def border_copy(q, side):
        to = z + span_first if side == 0 else z - span_first
        cols = pl.ds(q * piece, piece)
        return pltpu.make_async_remote_copy(
            src_ref=m.at[1, :, cols],
            dst_ref=m.at[side, :, cols],
            send_sem=b_send.at[q, side // 2],
            recv_sem=b_recv.at[q, side // 2],
            device_id={"seq": to},
            device_id_type=MESH,
        )

    sends_up = z + span_first < count
    sends_down = z >= span_first

    for q in range(CHUNKS):
        each_share(q, lambda copy: copy.wait_recv(), True)
        cols = pl.ds(q * piece, piece)

        def store_middle(rows, value):
            m[1, rows, cols] = value

        layer(
            w2, e, valid(0, z, span_second), valid(2, z, span_second), cols,
            u2_ref, slope2, scale2, dg, store_middle,
        )

        @pl.when(sends_up)
        def _():
            border_copy(q, 0).start()

        @pl.when(sends_down)
        def _():
            border_copy(q, 2).start()

    def tap_terms(tap, side):
        @pl.loop(0, chan // BLOCK)
        def _(step):
            start = pl.multiple_of(step * BLOCK, BLOCK)
            part = lax.dot_general(
                gelu1[pl.ds(start, BLOCK), :], m[side],
                (((1,), (1,)), ((), ())), preferred_element_type=F32,
            )
            terms[pl.ds(pl.multiple_of(tap * chan + start, BLOCK), BLOCK), :] = part * factor

    def border_terms(tap, side, has):
        @pl.when(has)
        def _():
            for q in range(CHUNKS):
                border_copy(q, side).wait_recv()
            tap_terms(tap, side)

        @pl.when(jnp.logical_not(has))
        def _():
            terms[pl.ds(tap * chan, chan), :] = jnp.zeros((chan, terms.shape[1]), F32)

    tap_terms(1, 1)
    if early is not None:
        reduction = Reduction(z, x, core, sib, across, early, terms, more)
        reduction.start_early()
    border_terms(0, 2, sends_up)
    border_terms(2, 0, sends_down)
    load1.wait()

    def store_total(cols):
        def store(rows, value):
            grad_ref[rows, cols] = value
        return store

    def result_copy(q):
        cols = pl.ds(q * piece, piece)
        return pltpu.make_async_copy(grad_ref.at[:, cols], grad_hbm.at[:, cols], w_sem.at[7 + q])

    def first_layer(q):
        cols = pl.ds(q * piece, piece)
        layer(
            w1, m, sends_down, sends_up, cols,
            u1_ref, slope1, scale1, dg, store_total(cols),
        )
        result_copy(q).start()

    if early is not None:
        def first_layer_part(part):
            for q in range(part * CHUNKS // 2, (part + 1) * CHUNKS // 2):
                first_layer(q)

        reduction.run(first_layer_part, wgrad_hbm)
    else:
        for q in range(CHUNKS):
            first_layer(q)
        terms_out = pltpu.make_async_copy(terms, wgrad_hbm, w_sem.at[0])
        terms_out.start()
        terms_out.wait()
    for q in range(CHUNKS):
        result_copy(q).wait()

    for q in range(CHUNKS):
        each_share(q, lambda copy: copy.wait_send(), False)

        @pl.when(sends_up)
        def _():
            border_copy(q, 0).wait_send()

        @pl.when(sends_down)
        def _():
            border_copy(q, 2).wait_send()


class Reduction:
    def __init__(self, z, x, core, sib, across, early, terms, refs):
        self.z, self.x, self.core, self.sib, self.across = z, x, core, sib, across
        self.terms = terms
        (self.core_out, self.core_in, self.x_out, self.x_in, self.z_out, self.z_in, self.kept, self.final,
         self.core_send, self.core_recv, self.x_send, self.x_recv,
         self.z_send, self.z_recv, self.f_send, self.f_recv, self.o_sem) = refs
        self.each, self.half = self.core_out.shape[1:]
        self.mine = pl.ds(pl.multiple_of(core * self.half, 128), self.half)
        self.theirs = pl.ds(pl.multiple_of((1 - core) * self.half, 128), self.half)
        self.early_block = early[1] + x * (early[0] - early[1])
        self.early_unit = flip(self.early_block, z % 2, z // 2)

    def block(self, k):
        return flip(self.z, k % 2, k // 2)

    def rows(self, turn, block, part):
        return pl.ds(pl.multiple_of(((block * 2 + part) * 2 + turn) * self.each, 16), self.each)

    def core_copy(self, slot):
        return pltpu.make_async_remote_copy(
            src_ref=self.core_out.at[slot], dst_ref=self.core_in.at[slot],
            send_sem=self.core_send.at[slot], recv_sem=self.core_recv.at[slot],
            device_id={"batch": self.sib}, device_id_type=MESH,
        )

    def x_copy(self, k):
        return pltpu.make_async_remote_copy(
            src_ref=self.x_out.at[k], dst_ref=self.x_in.at[k],
            send_sem=self.x_send.at[k], recv_sem=self.x_recv.at[k],
            device_id={"batch": self.across}, device_id_type=MESH,
        )

    def z_copy(self, turn, kind):
        slot = turn * 3 + kind
        return pltpu.make_async_remote_copy(
            src_ref=self.z_out.at[slot], dst_ref=self.z_in.at[slot],
            send_sem=self.z_send.at[slot], recv_sem=self.z_recv.at[slot],
            device_id={"seq": self.block(2 if kind == 2 else 1)}, device_id_type=MESH,
        )

    def to_core(self, turn, slot, block, part):
        self.core_out[turn * 8 + slot] = self.terms[
            self.rows(turn, block, part), self.theirs
        ].astype(BF16)
        self.core_copy(turn * 8 + slot).start()

    def to_x(self, turn, k, block):
        self.core_copy(turn * 8 + k).wait_recv()
        own = self.terms[self.rows(turn, block, 1 - self.x), self.mine]
        total = own + self.core_in[turn * 8 + k].astype(F32)
        self.x_out[turn * 4 + k] = total.astype(BF16)
        self.x_copy(turn * 4 + k).start()

    def start_early(self):
        for turn in range(2):
            self.to_core(turn, self.early_unit, self.early_block, 1 - self.x)
        for turn in range(2):
            self.to_x(turn, self.early_unit, self.early_block)

    def stage(self, turn, k):
        self.core_copy(turn * 8 + 4 + k).wait_recv()
        self.x_copy(turn * 4 + k).wait_recv()
        own = self.terms[self.rows(turn, self.block(k), self.x), self.mine]
        total = own + self.core_in[turn * 8 + 4 + k].astype(F32)
        total = total + self.x_in[turn * 4 + k].astype(F32)
        if k == 2:
            self.z_copy(turn, 0).wait_recv()
            total = total + self.z_in[turn * 3].astype(F32)
        if k == 0:
            self.kept[turn] = total
        else:
            kind = {3: 0, 1: 1, 2: 2}[k]
            self.z_out[turn * 3 + kind] = total.astype(BF16)
            self.z_copy(turn, kind).start()

    def final_copy(self, turn, index, slot, to):
        place = self.final.at[slot, pl.ds(turn * self.each, self.each)]
        return pltpu.make_async_remote_copy(
            src_ref=place, dst_ref=place,
            send_sem=self.f_send.at[turn, index], recv_sem=self.f_recv.at[turn, index],
            device_id={"batch": to}, device_id_type=MESH,
        )

    def gather(self, turn):
        self.z_copy(turn, 1).wait_recv()
        total = self.kept[turn] + self.z_in[turn * 3 + 1].astype(F32)
        self.z_copy(turn, 2).wait_recv()
        total = total + self.z_in[turn * 3 + 2].astype(F32)
        me = self.x * 2 + self.core
        self.final[me, pl.ds(turn * self.each, self.each)] = total.astype(BF16)
        self.final_copy(turn, 0, me, self.across).start()
        self.final_copy(turn, 1, me, self.sib).start()

    def forward(self, turn):
        self.final_copy(turn, 0, self.across, self.across).wait_recv()
        self.final_copy(turn, 2, self.across, self.sib).start()

    def run(self, meanwhile, wgrad_hbm):
        units = (3, 2, 1, 0)
        for turn in range(2):
            for k in units:
                @pl.when(k != self.early_unit)
                def _():
                    self.to_core(turn, k, self.block(k), 1 - self.x)
        for turn in range(2):
            for k in units:
                @pl.when(k != self.early_unit)
                def _():
                    self.to_x(turn, k, self.block(k))
            for k in units:
                self.to_core(turn, 4 + k, self.block(k), self.x)
        meanwhile(0)
        self.stage(0, 3)
        self.stage(0, 2)
        meanwhile(1)
        self.stage(0, 1)
        self.stage(0, 0)
        self.stage(1, 3)
        self.stage(1, 2)
        self.gather(0)
        self.stage(1, 1)
        self.stage(1, 0)
        self.forward(0)
        self.gather(1)

        me, sib, across = self.x * 2 + self.core, self.sib, self.across
        last = (1 - self.x) * 2 + 1 - self.core

        def out_copy(slot):
            return pltpu.make_async_copy(
                self.final.at[slot], wgrad_hbm.at[slot], self.o_sem.at[slot]
            )

        out_copy(me).start()
        for turn in range(2):
            self.final_copy(turn, 1, sib, sib).wait_recv()
        out_copy(sib).start()
        self.forward(1)
        out_copy(across).start()
        for turn in range(2):
            self.final_copy(turn, 2, last, sib).wait_recv()
        out_copy(last).start()

        for turn in range(2):
            self.final_copy(turn, 0, me, across).wait_send()
            self.final_copy(turn, 1, me, sib).wait_send()
            self.final_copy(turn, 2, across, sib).wait_send()
            for kind in range(3):
                self.z_copy(turn, kind).wait_send()
        for slot in range(16):
            self.core_copy(slot).wait_send()
        for k in range(8):
            self.x_copy(k).wait_send()
        for slot in range(4):
            out_copy(slot).wait()


def flip(value, bit, high):
    low_part, high_part = value % 2, value // 2
    return 2 * (high_part + high - 2 * high_part * high) + low_part + bit - 2 * low_part * bit


def finish(grad_hbm, parts_hbm, grad_out, wgrad_out, grad, parts, wgrad, sems):
    each, half = parts.shape[1:]
    into = pltpu.make_async_copy(grad_hbm, grad, sems.at[0])
    parts_in = pltpu.make_async_copy(parts_hbm, parts, sems.at[1])
    parts_in.start()
    into.start()
    parts_in.wait()
    out = []
    for part in range(2):
        rows = pl.ds(part * each, each)
        for side in range(2):
            wgrad[rows, pl.ds(side * half, half)] = parts[part * 2 + side].astype(F32)
        out.append(pltpu.make_async_copy(wgrad.at[rows], wgrad_out.at[rows], sems.at[3 + part]))
        out[-1].start()
    into.wait()
    out.append(pltpu.make_async_copy(grad, grad_out, sems.at[2]))
    out[-1].start()
    for copy in out:
        copy.wait()


def on_device(seq, batch, head, u1, u2, w1, w2, c1, c2):
    chan, width = u1.shape[1:]
    out_chan = w1.shape[2]
    taps = w1.shape[0]
    total_rows = taps * chan
    factor = 1.0 / math.sqrt(u1.shape[0] * batch * width * seq)
    spans = (DILATION_FIRST // width, DILATION_SECOND // width)
    rows = total_rows // seq
    rows_each, half = rows // 2, out_chan // 2
    early = [
        [
            block for block in range(seq)
            if chan <= (2 * block + part) * rows_each <= 2 * chan - rows_each
        ][:1]
        for part in range(2)
    ]
    reduce = (
        seq == 4 and batch == 4 and rows % 64 == 0 and out_chan % 256 == 0 and all(early)
    )
    early = [blocks[0] for blocks in early] if reduce else None
    vmem = pl.BlockSpec(memory_space=pltpu.VMEM)
    anywhere = pl.BlockSpec(memory_space=pl.ANY)
    dma = pltpu.SemaphoreType.DMA
    scratch = [
        pltpu.VMEM((chan, width), BF16),
        pltpu.VMEM((chan, width), BF16),
        pltpu.VMEM((chan, width), BF16),
        pltpu.VMEM((chan, 128), F32),
        pltpu.VMEM((chan, 128), F32),
        pltpu.VMEM(w1.shape, BF16),
        pltpu.VMEM(w2.shape, BF16),
        pltpu.VMEM((3, chan, width), BF16),
        pltpu.VMEM((3, chan, width), BF16),
        pltpu.VMEM((chan, width), F32),
        pltpu.VMEM((chan, width), F32),
        pltpu.VMEM((1, width), F32),
        pltpu.VMEM((1, width), F32),
        pltpu.VMEM((chan, width), BF16),
        pltpu.VMEM((chan, width // CHUNKS), F32),
        pltpu.VMEM((total_rows, out_chan), F32),
        dma((7 + CHUNKS,)),
        dma((CHUNKS, seq - 1, 3)),
        dma((CHUNKS, seq - 1, 3)),
        dma((CHUNKS, 2)),
        dma((CHUNKS, 2)),
    ]
    if reduce:
        unit = rows_each // 2
        scratch += [
            pltpu.VMEM((16, unit, half), BF16),
            pltpu.VMEM((16, unit, half), BF16),
            pltpu.VMEM((8, unit, half), BF16),
            pltpu.VMEM((8, unit, half), BF16),
            pltpu.VMEM((6, unit, half), BF16),
            pltpu.VMEM((6, unit, half), BF16),
            pltpu.VMEM((2, unit, half), F32),
            pltpu.VMEM((4, rows_each, half), BF16),
            dma((16,)),
            dma((16,)),
            dma((8,)),
            dma((8,)),
            dma((6,)),
            dma((6,)),
            dma((2, 3)),
            dma((2, 3)),
            dma((4,)),
        ]
    grad, wgrad = pl.pallas_call(
        functools.partial(kernel, seq, spans, factor, early),
        out_shape=(
            jax.ShapeDtypeStruct((chan, width), BF16),
            jax.ShapeDtypeStruct((4, rows_each, half), BF16)
            if reduce else jax.ShapeDtypeStruct((total_rows, out_chan), F32),
        ),
        in_specs=[anywhere] * 5 + [vmem, vmem],
        out_specs=(anywhere, anywhere),
        scratch_shapes=scratch,
        compiler_params=pltpu.CompilerParams(
            collective_id=0, has_side_effects=True, vmem_limit_bytes=56 * 1024 * 1024
        ),
        cost_estimate=pl.CostEstimate(
            flops=18 * chan * out_chan * width, bytes_accessed=20_000_000, transcendentals=2 * chan * width
        ),
    )(head[0], u1[0], u2[0], w1, w2, c1, c2)
    if reduce:
        shapes = (
            jax.ShapeDtypeStruct(grad.shape, BF16),
            jax.ShapeDtypeStruct((rows, out_chan), F32),
        )
        grad, wgrad = pl.pallas_call(
            finish,
            out_shape=shapes,
            in_specs=[anywhere, anywhere],
            out_specs=(anywhere, anywhere),
            scratch_shapes=[
                pltpu.VMEM(grad.shape, BF16),
                pltpu.VMEM(wgrad.shape, BF16),
                pltpu.VMEM((rows, out_chan), F32),
                dma((5,)),
            ],
            compiler_params=pltpu.CompilerParams(vmem_limit_bytes=56 * 1024 * 1024),
        )(grad, wgrad)
    else:
        wgrad = lax.psum(lax.psum_scatter(wgrad, "seq", scatter_dimension=0, tiled=True), "batch")
    return grad[None], wgrad


def solution(mesh):
    in_specs = (
        P(("grp", "batch"), "seq", None),
        P(("grp", "batch"), None, "seq"),
        P(("grp", "batch"), None, "seq"),
        P(),
        P(),
        P(),
        P(),
    )
    out_specs = (P(("grp", "batch"), None, "seq"), P(("grp", "seq"), None))
    return jax.shard_map(
        functools.partial(on_device, mesh.shape["seq"], mesh.shape["batch"]),
        mesh=mesh, in_specs=in_specs, out_specs=out_specs, check_vma=False,
    )
```

```python
import functools
import math

import jax
import jax.numpy as jnp
from jax import lax
from jax.experimental import pallas as pl
from jax.experimental.pallas import tpu as pltpu
from jax.sharding import PartitionSpec as P

DILATION_FIRST = 512
DILATION_SECOND = 1024

EPS = 1e-06
SLOPE = math.sqrt(2.0 / math.pi)
CUBIC = 0.044715

F32 = jnp.float32
BF16 = jnp.bfloat16
MESH = pl.DeviceIdType.MESH
CHUNKS = 4
STRIP = 64
BLOCK = 768


def prepare(u_ref, gain_ref, slope_ref, scale_ref, gelu_ref):
    chan, width = u_ref.shape

    def square(step, total):
        rows = pl.ds(pl.multiple_of(step * STRIP, STRIP), STRIP)
        x = u_ref[rows, :].astype(F32)
        return total + jnp.sum(x * x, axis=0, keepdims=True)

    total = lax.fori_loop(0, chan // STRIP, square, jnp.zeros((1, width), F32))
    scale = lax.rsqrt(total / chan + EPS)
    scale_ref[...] = scale

    @pl.loop(0, chan // STRIP)
    def _(step):
        rows = pl.ds(pl.multiple_of(step * STRIP, STRIP), STRIP)
        gain = gain_ref[rows, 0:1]
        a = u_ref[rows, :].astype(F32) * scale * gain
        t = jnp.tanh(SLOPE * (a + CUBIC * a * a * a))
        slope = 0.5 * (1.0 + t) + 0.5 * a * (1.0 - t * t) * SLOPE * (1.0 + 3.0 * CUBIC * a * a)
        slope_ref[rows, :] = slope * gain
        if gelu_ref is not None:
            gelu_ref[rows, :] = (0.5 * a * (1.0 + t)).astype(BF16)


def layer(w_ref, e_ref, has_low, has_up, cols, u_ref, slope_ref, scale_ref, dg_ref, store):
    chan = u_ref.shape[0]
    width = cols.size

    def taps(tap, side, add):
        @pl.loop(0, chan // BLOCK)
        def _(step):
            rows = pl.ds(pl.multiple_of(step * BLOCK, BLOCK), BLOCK)
            part = jnp.dot(w_ref[tap, rows, :], e_ref[side, :, cols], preferred_element_type=F32)
            dg_ref[rows, :] = dg_ref[rows, :] + part if add else part

    taps(1, 1, False)

    @pl.when(has_low)
    def _():
        taps(2, 0, True)

    @pl.when(has_up)
    def _():
        taps(0, 2, True)

    def inner_step(step, total):
        rows = pl.ds(pl.multiple_of(step * STRIP, STRIP), STRIP)
        dn = dg_ref[rows, :] * slope_ref[rows, cols]
        dg_ref[rows, :] = dn
        return total + jnp.sum(dn * u_ref[rows, cols].astype(F32), axis=0, keepdims=True)

    inner = lax.fori_loop(0, chan // STRIP, inner_step, jnp.zeros((1, width), F32)) / chan
    scale = scale_ref[:, cols]
    cubed = scale * scale * scale * inner

    @pl.loop(0, chan // STRIP)
    def _(step):
        rows = pl.ds(pl.multiple_of(step * STRIP, STRIP), STRIP)
        dinput = scale * dg_ref[rows, :] - u_ref[rows, cols].astype(F32) * cubed
        store(rows, (e_ref[1, rows, cols].astype(F32) + dinput).astype(BF16))


def kernel(
    count, spans, factor, early,
    h_ref, u1_hbm, u2_hbm, w1_hbm, w2_hbm, c1_ref, c2_ref,
    grad_hbm, wgrad_hbm,
    u1_ref, u2_ref, grad_ref, gain1, gain2, w1, w2, e, m, slope1, slope2, scale1, scale2, gelu1, dg, terms,
    w_sem, a_send, a_recv, b_send, b_recv, *more,
):
    span_first, span_second = spans
    z = lax.axis_index("seq")
    chan, width = u1_ref.shape
    share = h_ref.shape[0]
    piece = width // CHUNKS

    load2 = pltpu.make_async_copy(w2_hbm, w2, w_sem.at[0])
    load1 = pltpu.make_async_copy(w1_hbm, w1, w_sem.at[1])
    load_u2 = pltpu.make_async_copy(u2_hbm, u2_ref, w_sem.at[2])
    load_u1 = pltpu.make_async_copy(u1_hbm, u1_ref, w_sem.at[3])

    offsets = sorted(range(1, count), key=lambda j: -min(j, count - j))
    barrier = pltpu.get_barrier_semaphore()
    partners = [{"seq": lax.rem(z + j, count)} for j in offsets]
    if early is not None:
        b = lax.axis_index("batch")
        x, core = b // 2, b % 2
        sib, across = x * 2 + 1 - core, (1 - x) * 2 + core
        partners += [{"batch": sib}, {"batch": across}]
    for partner in partners:
        pl.semaphore_signal(barrier, inc=1, device_id=partner, device_id_type=MESH)
    pl.semaphore_wait(barrier, len(partners))

    def valid(side, owner, span):
        if side == 0:
            return owner >= span
        return owner + span < count

    def share_copy(q, j, side, source, dest):
        shift = (side - 1) * span_second
        at = pl.multiple_of((dest + shift) * width, 128) + q * piece
        return pltpu.make_async_remote_copy(
            src_ref=h_ref.at[:, pl.ds(pl.multiple_of(at, 128), piece)],
            dst_ref=e.at[side, pl.ds(pl.multiple_of(source * share, 16), share), pl.ds(q * piece, piece)],
            send_sem=a_send.at[q, j - 1, side],
            recv_sem=a_recv.at[q, j - 1, side],
            device_id={"seq": dest},
            device_id_type=MESH,
        )

    def each_share(q, act, incoming):
        for j in offsets:
            source = lax.rem(z - j + count, count) if incoming else z
            dest = z if incoming else lax.rem(z + j, count)
            for side in (0, 1, 2):
                def go(side=side):
                    act(share_copy(q, j, side, source, dest))
                if side == 1:
                    go()
                else:
                    pl.when(valid(side, dest, span_second))(go)

    for q in range(CHUNKS):
        each_share(q, lambda copy: copy.start(), False)

    own = pl.ds(pl.multiple_of(z * share, 16), share)

    def each_own(act):
        for side in (0, 1, 2):
            def keep(side=side):
                at = pl.multiple_of((z + (side - 1) * span_second) * width, 128)
                act(pltpu.make_async_copy(
                    h_ref.at[:, pl.ds(at, width)], e.at[side, own, :], w_sem.at[4 + side]
                ))
            if side == 1:
                keep()
            else:
                pl.when(valid(side, z, span_second))(keep)

    load_u2.start()
    load_u1.start()
    each_own(lambda copy: copy.start())
    load2.start()
    load1.start()
    for gain, row in ((gain1, c1_ref), (gain2, c2_ref)):
        gain[...] = jnp.transpose(jnp.broadcast_to(row[...].reshape(1, chan), (gain.shape[1], chan)))
    load_u2.wait()
    prepare(u2_ref, gain2, slope2, scale2, None)
    load_u1.wait()
    prepare(u1_ref, gain1, slope1, scale1, gelu1)
    load2.wait()
    each_own(lambda copy: copy.wait())

    def border_copy(q, side):
        to = z + span_first if side == 0 else z - span_first
        cols = pl.ds(q * piece, piece)
        return pltpu.make_async_remote_copy(
            src_ref=m.at[1, :, cols],
            dst_ref=m.at[side, :, cols],
            send_sem=b_send.at[q, side // 2],
            recv_sem=b_recv.at[q, side // 2],
            device_id={"seq": to},
            device_id_type=MESH,
        )

    sends_up = z + span_first < count
    sends_down = z >= span_first

    for q in range(CHUNKS):
        each_share(q, lambda copy: copy.wait_recv(), True)
        cols = pl.ds(q * piece, piece)

        def store_middle(rows, value):
            m[1, rows, cols] = value

        layer(
            w2, e, valid(0, z, span_second), valid(2, z, span_second), cols,
            u2_ref, slope2, scale2, dg, store_middle,
        )

        @pl.when(sends_up)
        def _():
            border_copy(q, 0).start()

        @pl.when(sends_down)
        def _():
            border_copy(q, 2).start()

    def tap_terms(tap, side):
        @pl.loop(0, chan // BLOCK)
        def _(step):
            start = pl.multiple_of(step * BLOCK, BLOCK)
            part = lax.dot_general(
                gelu1[pl.ds(start, BLOCK), :], m[side],
                (((1,), (1,)), ((), ())), preferred_element_type=F32,
            )
            terms[pl.ds(pl.multiple_of(tap * chan + start, BLOCK), BLOCK), :] = part * factor

    def border_terms(tap, side, has):
        @pl.when(has)
        def _():
            tap_terms(tap, side)

        @pl.when(jnp.logical_not(has))
        def _():
            terms[pl.ds(tap * chan, chan), :] = jnp.zeros((chan, terms.shape[1]), F32)

    def store_total(cols):
        def store(rows, value):
            grad_ref[rows, cols] = value
        return store

    def result_copy(q):
        cols = pl.ds(q * piece, piece)
        return pltpu.make_async_copy(grad_ref.at[:, cols], grad_hbm.at[:, cols], w_sem.at[7 + q])

    def first_layer(q):
        cols = pl.ds(q * piece, piece)
        layer(
            w1, m, sends_down, sends_up, cols,
            u1_ref, slope1, scale1, dg, store_total(cols),
        )
        result_copy(q).start()

    tap_terms(1, 1)
    if early is not None:
        reduction = Reduction(z, x, core, sib, across, early, terms, more)
        reduction.start_early()
    load1.wait()
    for q in range(CHUNKS):
        pl.when(sends_down)(border_copy(q, 0).wait_recv)
        pl.when(sends_up)(border_copy(q, 2).wait_recv)
        if q < CHUNKS - 1:
            first_layer(q)
    border_terms(0, 2, sends_up)
    border_terms(2, 0, sends_down)

    if early is not None:
        reduction.run(functools.partial(first_layer, CHUNKS - 1), wgrad_hbm)
    else:
        first_layer(CHUNKS - 1)
        terms_out = pltpu.make_async_copy(terms, wgrad_hbm, w_sem.at[0])
        terms_out.start()
        terms_out.wait()
    for q in range(CHUNKS):
        result_copy(q).wait()

    for q in range(CHUNKS):
        each_share(q, lambda copy: copy.wait_send(), False)

        @pl.when(sends_up)
        def _():
            border_copy(q, 0).wait_send()

        @pl.when(sends_down)
        def _():
            border_copy(q, 2).wait_send()


class Reduction:
    def __init__(self, z, x, core, sib, across, early, terms, refs):
        self.z, self.x, self.core, self.sib, self.across = z, x, core, sib, across
        self.terms = terms
        (self.core_out, self.core_in, self.x_out, self.x_in, self.z_out, self.z_in, self.kept, self.final,
         self.core_send, self.core_recv, self.x_send, self.x_recv,
         self.z_send, self.z_recv, self.f_send, self.f_recv, self.o_sem) = refs
        self.each, self.half = self.core_out.shape[1:]
        self.mine = pl.ds(pl.multiple_of(core * self.half, 128), self.half)
        self.theirs = pl.ds(pl.multiple_of((1 - core) * self.half, 128), self.half)
        self.early_block = early[1] + x * (early[0] - early[1])
        self.early_unit = flip(self.early_block, z % 2, z // 2)

    def block(self, k):
        return flip(self.z, k % 2, k // 2)

    def rows(self, turn, block, part):
        return pl.ds(pl.multiple_of(((block * 2 + part) * 2 + turn) * self.each, 16), self.each)

    def core_copy(self, slot):
        return pltpu.make_async_remote_copy(
            src_ref=self.core_out.at[slot], dst_ref=self.core_in.at[slot],
            send_sem=self.core_send.at[slot], recv_sem=self.core_recv.at[slot],
            device_id={"batch": self.sib}, device_id_type=MESH,
        )

    def x_copy(self, k):
        return pltpu.make_async_remote_copy(
            src_ref=self.x_out.at[k], dst_ref=self.x_in.at[k],
            send_sem=self.x_send.at[k], recv_sem=self.x_recv.at[k],
            device_id={"batch": self.across}, device_id_type=MESH,
        )

    def z_copy(self, turn, kind):
        slot = turn * 3 + kind
        return pltpu.make_async_remote_copy(
            src_ref=self.z_out.at[slot], dst_ref=self.z_in.at[slot],
            send_sem=self.z_send.at[slot], recv_sem=self.z_recv.at[slot],
            device_id={"seq": self.block(2 if kind == 2 else 1)}, device_id_type=MESH,
        )

    def to_core(self, turn, slot, block, part):
        self.core_out[turn * 8 + slot] = self.terms[
            self.rows(turn, block, part), self.theirs
        ].astype(BF16)
        self.core_copy(turn * 8 + slot).start()

    def to_x(self, turn, k, block):
        self.core_copy(turn * 8 + k).wait_recv()
        own = self.terms[self.rows(turn, block, 1 - self.x), self.mine]
        total = own + self.core_in[turn * 8 + k].astype(F32)
        self.x_out[turn * 4 + k] = total.astype(BF16)
        self.x_copy(turn * 4 + k).start()

    def start_early(self):
        for turn in range(2):
            self.to_core(turn, self.early_unit, self.early_block, 1 - self.x)
        for turn in range(2):
            self.to_x(turn, self.early_unit, self.early_block)

    def stage(self, turn, k):
        self.core_copy(turn * 8 + 4 + k).wait_recv()
        self.x_copy(turn * 4 + k).wait_recv()
        own = self.terms[self.rows(turn, self.block(k), self.x), self.mine]
        total = own + self.core_in[turn * 8 + 4 + k].astype(F32)
        total = total + self.x_in[turn * 4 + k].astype(F32)
        if k == 2:
            self.z_copy(turn, 0).wait_recv()
            total = total + self.z_in[turn * 3].astype(F32)
        if k == 0:
            self.kept[turn] = total
        else:
            kind = {3: 0, 1: 1, 2: 2}[k]
            self.z_out[turn * 3 + kind] = total.astype(BF16)
            self.z_copy(turn, kind).start()

    def final_copy(self, turn, index, slot, to):
        place = self.final.at[slot, pl.ds(turn * self.each, self.each)]
        return pltpu.make_async_remote_copy(
            src_ref=place, dst_ref=place,
            send_sem=self.f_send.at[turn, index], recv_sem=self.f_recv.at[turn, index],
            device_id={"batch": to}, device_id_type=MESH,
        )

    def gather(self, turn):
        self.z_copy(turn, 1).wait_recv()
        total = self.kept[turn] + self.z_in[turn * 3 + 1].astype(F32)
        self.z_copy(turn, 2).wait_recv()
        total = total + self.z_in[turn * 3 + 2].astype(F32)
        me = self.x * 2 + self.core
        self.final[me, pl.ds(turn * self.each, self.each)] = total.astype(BF16)
        self.final_copy(turn, 0, me, self.across).start()
        self.final_copy(turn, 1, me, self.sib).start()

    def forward(self, turn):
        self.final_copy(turn, 0, self.across, self.across).wait_recv()
        self.final_copy(turn, 2, self.across, self.sib).start()

    def run(self, meanwhile, wgrad_hbm):
        units = (3, 2, 1, 0)
        for turn in range(2):
            for k in units:
                @pl.when(k != self.early_unit)
                def _():
                    self.to_core(turn, k, self.block(k), 1 - self.x)
        for turn in range(2):
            for k in units:
                @pl.when(k != self.early_unit)
                def _():
                    self.to_x(turn, k, self.block(k))
            for k in units:
                self.to_core(turn, 4 + k, self.block(k), self.x)
        meanwhile()
        self.stage(0, 3)
        self.stage(0, 2)
        self.stage(0, 1)
        self.stage(0, 0)
        self.stage(1, 3)
        self.stage(1, 2)
        self.gather(0)
        self.stage(1, 1)
        self.stage(1, 0)
        self.forward(0)
        self.gather(1)

        me, sib, across = self.x * 2 + self.core, self.sib, self.across
        last = (1 - self.x) * 2 + 1 - self.core

        def out_copy(slot):
            return pltpu.make_async_copy(
                self.final.at[slot], wgrad_hbm.at[slot], self.o_sem.at[slot]
            )

        out_copy(me).start()
        for turn in range(2):
            self.final_copy(turn, 1, sib, sib).wait_recv()
        out_copy(sib).start()
        self.forward(1)
        out_copy(across).start()
        for turn in range(2):
            self.final_copy(turn, 2, last, sib).wait_recv()
        out_copy(last).start()

        for turn in range(2):
            self.final_copy(turn, 0, me, across).wait_send()
            self.final_copy(turn, 1, me, sib).wait_send()
            self.final_copy(turn, 2, across, sib).wait_send()
            for kind in range(3):
                self.z_copy(turn, kind).wait_send()
        for slot in range(16):
            self.core_copy(slot).wait_send()
        for k in range(8):
            self.x_copy(k).wait_send()
        for slot in range(4):
            out_copy(slot).wait()


def flip(value, bit, high):
    low_part, high_part = value % 2, value // 2
    return 2 * (high_part + high - 2 * high_part * high) + low_part + bit - 2 * low_part * bit


def finish(grad_hbm, parts_hbm, grad_out, wgrad_out, grad, parts, wgrad, sems):
    each, half = parts.shape[1:]
    into = pltpu.make_async_copy(grad_hbm, grad, sems.at[0])
    parts_in = pltpu.make_async_copy(parts_hbm, parts, sems.at[1])
    parts_in.start()
    into.start()
    parts_in.wait()
    out = []
    for part in range(2):
        rows = pl.ds(part * each, each)
        for side in range(2):
            wgrad[rows, pl.ds(side * half, half)] = parts[part * 2 + side].astype(F32)
        out.append(pltpu.make_async_copy(wgrad.at[rows], wgrad_out.at[rows], sems.at[3 + part]))
        out[-1].start()
    into.wait()
    out.append(pltpu.make_async_copy(grad, grad_out, sems.at[2]))
    out[-1].start()
    for copy in out:
        copy.wait()


def on_device(seq, batch, head, u1, u2, w1, w2, c1, c2):
    chan, width = u1.shape[1:]
    out_chan = w1.shape[2]
    taps = w1.shape[0]
    total_rows = taps * chan
    factor = 1.0 / math.sqrt(u1.shape[0] * batch * width * seq)
    spans = (DILATION_FIRST // width, DILATION_SECOND // width)
    rows = total_rows // seq
    rows_each, half = rows // 2, out_chan // 2
    early = [
        [
            block for block in range(seq)
            if chan <= (2 * block + part) * rows_each <= 2 * chan - rows_each
        ][:1]
        for part in range(2)
    ]
    reduce = (
        seq == 4 and batch == 4 and rows % 64 == 0 and out_chan % 256 == 0 and all(early)
    )
    early = [blocks[0] for blocks in early] if reduce else None
    vmem = pl.BlockSpec(memory_space=pltpu.VMEM)
    anywhere = pl.BlockSpec(memory_space=pl.ANY)
    dma = pltpu.SemaphoreType.DMA
    scratch = [
        pltpu.VMEM((chan, width), BF16),
        pltpu.VMEM((chan, width), BF16),
        pltpu.VMEM((chan, width), BF16),
        pltpu.VMEM((chan, 128), F32),
        pltpu.VMEM((chan, 128), F32),
        pltpu.VMEM(w1.shape, BF16),
        pltpu.VMEM(w2.shape, BF16),
        pltpu.VMEM((3, chan, width), BF16),
        pltpu.VMEM((3, chan, width), BF16),
        pltpu.VMEM((chan, width), F32),
        pltpu.VMEM((chan, width), F32),
        pltpu.VMEM((1, width), F32),
        pltpu.VMEM((1, width), F32),
        pltpu.VMEM((chan, width), BF16),
        pltpu.VMEM((chan, width // CHUNKS), F32),
        pltpu.VMEM((total_rows, out_chan), F32),
        dma((7 + CHUNKS,)),
        dma((CHUNKS, seq - 1, 3)),
        dma((CHUNKS, seq - 1, 3)),
        dma((CHUNKS, 2)),
        dma((CHUNKS, 2)),
    ]
    if reduce:
        unit = rows_each // 2
        scratch += [
            pltpu.VMEM((16, unit, half), BF16),
            pltpu.VMEM((16, unit, half), BF16),
            pltpu.VMEM((8, unit, half), BF16),
            pltpu.VMEM((8, unit, half), BF16),
            pltpu.VMEM((6, unit, half), BF16),
            pltpu.VMEM((6, unit, half), BF16),
            pltpu.VMEM((2, unit, half), F32),
            pltpu.VMEM((4, rows_each, half), BF16),
            dma((16,)),
            dma((16,)),
            dma((8,)),
            dma((8,)),
            dma((6,)),
            dma((6,)),
            dma((2, 3)),
            dma((2, 3)),
            dma((4,)),
        ]
    grad, wgrad = pl.pallas_call(
        functools.partial(kernel, seq, spans, factor, early),
        out_shape=(
            jax.ShapeDtypeStruct((chan, width), BF16),
            jax.ShapeDtypeStruct((4, rows_each, half), BF16)
            if reduce else jax.ShapeDtypeStruct((total_rows, out_chan), F32),
        ),
        in_specs=[anywhere] * 5 + [vmem, vmem],
        out_specs=(anywhere, anywhere),
        scratch_shapes=scratch,
        compiler_params=pltpu.CompilerParams(
            collective_id=0, has_side_effects=True, vmem_limit_bytes=56 * 1024 * 1024
        ),
        cost_estimate=pl.CostEstimate(
            flops=18 * chan * out_chan * width, bytes_accessed=20_000_000, transcendentals=2 * chan * width
        ),
    )(head[0], u1[0], u2[0], w1, w2, c1, c2)
    if reduce:
        shapes = (
            jax.ShapeDtypeStruct(grad.shape, BF16),
            jax.ShapeDtypeStruct((rows, out_chan), F32),
        )
        grad, wgrad = pl.pallas_call(
            finish,
            out_shape=shapes,
            in_specs=[anywhere, anywhere],
            out_specs=(anywhere, anywhere),
            scratch_shapes=[
                pltpu.VMEM(grad.shape, BF16),
                pltpu.VMEM(wgrad.shape, BF16),
                pltpu.VMEM((rows, out_chan), F32),
                dma((5,)),
            ],
            compiler_params=pltpu.CompilerParams(vmem_limit_bytes=56 * 1024 * 1024),
        )(grad, wgrad)
    else:
        wgrad = lax.psum(lax.psum_scatter(wgrad, "seq", scatter_dimension=0, tiled=True), "batch")
    return grad[None], wgrad


def solution(mesh):
    in_specs = (
        P(("grp", "batch"), "seq", None),
        P(("grp", "batch"), None, "seq"),
        P(("grp", "batch"), None, "seq"),
        P(),
        P(),
        P(),
        P(),
    )
    out_specs = (P(("grp", "batch"), None, "seq"), P(("grp", "seq"), None))
    return jax.shard_map(
        functools.partial(on_device, mesh.shape["seq"], mesh.shape["batch"]),
        mesh=mesh, in_specs=in_specs, out_specs=out_specs, check_vma=False,
    )
```

```python
import functools
import math

import jax
import jax.numpy as jnp
from jax import lax
from jax.experimental import pallas as pl
from jax.experimental.pallas import tpu as pltpu
from jax.sharding import PartitionSpec as P

DILATION_FIRST = 512
DILATION_SECOND = 1024

EPS = 1e-06
SLOPE = math.sqrt(2.0 / math.pi)
CUBIC = 0.044715

F32 = jnp.float32
BF16 = jnp.bfloat16
MESH = pl.DeviceIdType.MESH
CHUNKS = 4
STRIP = 64
BLOCK = 768


def prepare(u_ref, gain_ref, slope_ref, scale_ref, gelu_ref):
    chan, width = u_ref.shape

    def square(step, total):
        rows = pl.ds(pl.multiple_of(step * STRIP, STRIP), STRIP)
        x = u_ref[rows, :].astype(F32)
        return total + jnp.sum(x * x, axis=0, keepdims=True)

    total = lax.fori_loop(0, chan // STRIP, square, jnp.zeros((1, width), F32))
    scale = lax.rsqrt(total / chan + EPS)
    scale_ref[...] = scale

    @pl.loop(0, chan // STRIP)
    def _(step):
        rows = pl.ds(pl.multiple_of(step * STRIP, STRIP), STRIP)
        gain = gain_ref[rows, 0:1]
        a = u_ref[rows, :].astype(F32) * scale * gain
        t = jnp.tanh(SLOPE * (a + CUBIC * a * a * a))
        slope = 0.5 * (1.0 + t) + 0.5 * a * (1.0 - t * t) * SLOPE * (1.0 + 3.0 * CUBIC * a * a)
        slope_ref[rows, :] = slope * gain
        if gelu_ref is not None:
            gelu_ref[rows, :] = (0.5 * a * (1.0 + t)).astype(BF16)


def layer(w_ref, e_ref, has_low, has_up, cols, u_ref, slope_ref, scale_ref, dg_ref, store):
    chan = u_ref.shape[0]
    width = cols.size

    def taps(tap, side, add):
        @pl.loop(0, chan // BLOCK)
        def _(step):
            rows = pl.ds(pl.multiple_of(step * BLOCK, BLOCK), BLOCK)
            part = jnp.dot(w_ref[tap, rows, :], e_ref[side, :, cols], preferred_element_type=F32)
            dg_ref[rows, :] = dg_ref[rows, :] + part if add else part

    taps(1, 1, False)

    @pl.when(has_low)
    def _():
        taps(2, 0, True)

    @pl.when(has_up)
    def _():
        taps(0, 2, True)

    def inner_step(step, total):
        rows = pl.ds(pl.multiple_of(step * STRIP, STRIP), STRIP)
        dn = dg_ref[rows, :] * slope_ref[rows, cols]
        dg_ref[rows, :] = dn
        return total + jnp.sum(dn * u_ref[rows, cols].astype(F32), axis=0, keepdims=True)

    inner = lax.fori_loop(0, chan // STRIP, inner_step, jnp.zeros((1, width), F32)) / chan
    scale = scale_ref[:, cols]
    cubed = scale * scale * scale * inner

    @pl.loop(0, chan // STRIP)
    def _(step):
        rows = pl.ds(pl.multiple_of(step * STRIP, STRIP), STRIP)
        dinput = scale * dg_ref[rows, :] - u_ref[rows, cols].astype(F32) * cubed
        store(rows, (e_ref[1, rows, cols].astype(F32) + dinput).astype(BF16))


def kernel(
    count, spans, factor, early,
    h_ref, u1_hbm, u2_hbm, w1_hbm, w2_hbm, c1_ref, c2_ref,
    grad_hbm, wgrad_hbm,
    u1_ref, u2_ref, grad_ref, gain1, gain2, w1, w2, e, m, slope1, slope2, scale1, scale2, gelu1, dg, terms,
    w_sem, a_send, a_recv, b_send, b_recv, *more,
):
    span_first, span_second = spans
    z = lax.axis_index("seq")
    chan, width = u1_ref.shape
    share = h_ref.shape[0]
    piece = width // CHUNKS

    load2 = pltpu.make_async_copy(w2_hbm, w2, w_sem.at[0])
    load1 = pltpu.make_async_copy(w1_hbm, w1, w_sem.at[1])
    load_u2 = pltpu.make_async_copy(u2_hbm, u2_ref, w_sem.at[2])
    load_u1 = pltpu.make_async_copy(u1_hbm, u1_ref, w_sem.at[3])

    offsets = sorted(range(1, count), key=lambda j: -min(j, count - j))
    barrier = pltpu.get_barrier_semaphore()
    partners = [{"seq": lax.rem(z + j, count)} for j in offsets]
    if early is not None:
        b = lax.axis_index("batch")
        x, core = b // 2, b % 2
        sib, across = x * 2 + 1 - core, (1 - x) * 2 + core
        partners += [{"batch": sib}, {"batch": across}]
    for partner in partners:
        pl.semaphore_signal(barrier, inc=1, device_id=partner, device_id_type=MESH)
    pl.semaphore_wait(barrier, len(partners))

    def valid(side, owner, span):
        if side == 0:
            return owner >= span
        return owner + span < count

    def share_copy(q, j, side, source, dest):
        shift = (side - 1) * span_second
        at = pl.multiple_of((dest + shift) * width, 128) + q * piece
        return pltpu.make_async_remote_copy(
            src_ref=h_ref.at[:, pl.ds(pl.multiple_of(at, 128), piece)],
            dst_ref=e.at[side, pl.ds(pl.multiple_of(source * share, 16), share), pl.ds(q * piece, piece)],
            send_sem=a_send.at[q, j - 1, side],
            recv_sem=a_recv.at[q, j - 1, side],
            device_id={"seq": dest},
            device_id_type=MESH,
        )

    def each_share(q, act, incoming):
        for j in offsets:
            source = lax.rem(z - j + count, count) if incoming else z
            dest = z if incoming else lax.rem(z + j, count)
            for side in (0, 1, 2):
                def go(side=side):
                    act(share_copy(q, j, side, source, dest))
                if side == 1:
                    go()
                else:
                    pl.when(valid(side, dest, span_second))(go)

    for q in range(CHUNKS):
        each_share(q, lambda copy: copy.start(), False)

    own = pl.ds(pl.multiple_of(z * share, 16), share)

    def each_own(act):
        for side in (0, 1, 2):
            def keep(side=side):
                at = pl.multiple_of((z + (side - 1) * span_second) * width, 128)
                act(pltpu.make_async_copy(
                    h_ref.at[:, pl.ds(at, width)], e.at[side, own, :], w_sem.at[4 + side]
                ))
            if side == 1:
                keep()
            else:
                pl.when(valid(side, z, span_second))(keep)

    load_u2.start()
    load_u1.start()
    each_own(lambda copy: copy.start())
    load2.start()
    load1.start()
    for gain, row in ((gain1, c1_ref), (gain2, c2_ref)):
        gain[...] = jnp.transpose(jnp.broadcast_to(row[...].reshape(1, chan), (gain.shape[1], chan)))
    load_u2.wait()
    prepare(u2_ref, gain2, slope2, scale2, None)
    load_u1.wait()
    prepare(u1_ref, gain1, slope1, scale1, gelu1)
    load2.wait()
    each_own(lambda copy: copy.wait())

    def border_copy(q, side):
        to = z + span_first if side == 0 else z - span_first
        cols = pl.ds(q * piece, piece)
        return pltpu.make_async_remote_copy(
            src_ref=m.at[1, :, cols],
            dst_ref=m.at[side, :, cols],
            send_sem=b_send.at[q, side // 2],
            recv_sem=b_recv.at[q, side // 2],
            device_id={"seq": to},
            device_id_type=MESH,
        )

    sends_up = z + span_first < count
    sends_down = z >= span_first

    for q in range(CHUNKS):
        each_share(q, lambda copy: copy.wait_recv(), True)
        cols = pl.ds(q * piece, piece)

        def store_middle(rows, value):
            m[1, rows, cols] = value

        layer(
            w2, e, valid(0, z, span_second), valid(2, z, span_second), cols,
            u2_ref, slope2, scale2, dg, store_middle,
        )

        @pl.when(sends_up)
        def _():
            border_copy(q, 0).start()

        @pl.when(sends_down)
        def _():
            border_copy(q, 2).start()

    def tap_terms(tap, side, cols, add):
        part = lax.dot_general(
            gelu1[:, cols], m[side, :, cols],
            (((1,), (1,)), ((), ())), preferred_element_type=F32,
        ) * factor
        rows = pl.ds(tap * chan, chan)
        terms[rows, :] = terms[rows, :] + part if add else part

    def border_terms(tap, side, has, cols, add):
        @pl.when(has)
        def _():
            tap_terms(tap, side, cols, add)

        if not add:
            @pl.when(jnp.logical_not(has))
            def _():
                terms[pl.ds(tap * chan, chan), :] = jnp.zeros((chan, terms.shape[1]), F32)

    def store_total(cols):
        def store(rows, value):
            grad_ref[rows, cols] = value
        return store

    def result_copy(q):
        cols = pl.ds(q * piece, piece)
        return pltpu.make_async_copy(grad_ref.at[:, cols], grad_hbm.at[:, cols], w_sem.at[7 + q])

    def first_layer(q):
        cols = pl.ds(q * piece, piece)
        layer(
            w1, m, sends_down, sends_up, cols,
            u1_ref, slope1, scale1, dg, store_total(cols),
        )
        result_copy(q).start()

    tap_terms(1, 1, pl.ds(0, width), False)
    if early is not None:
        reduction = Reduction(z, x, core, sib, across, early, terms, more)
        reduction.start_early()
    load1.wait()
    for q in range(CHUNKS):
        pl.when(sends_down)(border_copy(q, 0).wait_recv)
        pl.when(sends_up)(border_copy(q, 2).wait_recv)
        if q < CHUNKS - 2:
            first_layer(q)
        else:
            add = q == CHUNKS - 1
            cols = pl.ds(q * piece, piece) if add else pl.ds(0, (CHUNKS - 1) * piece)
            border_terms(0, 2, sends_up, cols, add)
            border_terms(2, 0, sends_down, cols, add)

    if early is not None:
        reduction.run(first_layer, wgrad_hbm)
    else:
        first_layer(CHUNKS - 2)
        first_layer(CHUNKS - 1)
        terms_out = pltpu.make_async_copy(terms, wgrad_hbm, w_sem.at[0])
        terms_out.start()
        terms_out.wait()
    for q in range(CHUNKS):
        result_copy(q).wait()

    for q in range(CHUNKS):
        each_share(q, lambda copy: copy.wait_send(), False)

        @pl.when(sends_up)
        def _():
            border_copy(q, 0).wait_send()

        @pl.when(sends_down)
        def _():
            border_copy(q, 2).wait_send()


class Reduction:
    def __init__(self, z, x, core, sib, across, early, terms, refs):
        self.z, self.x, self.core, self.sib, self.across = z, x, core, sib, across
        self.terms = terms
        (self.core_out, self.core_in, self.x_out, self.x_in, self.z_out, self.z_in, self.kept, self.final,
         self.core_send, self.core_recv, self.x_send, self.x_recv,
         self.z_send, self.z_recv, self.f_send, self.f_recv, self.o_sem) = refs
        self.each, self.half = self.core_out.shape[1:]
        self.mine = pl.ds(pl.multiple_of(core * self.half, 128), self.half)
        self.theirs = pl.ds(pl.multiple_of((1 - core) * self.half, 128), self.half)
        self.early_block = early[1] + x * (early[0] - early[1])
        self.early_unit = flip(self.early_block, z % 2, z // 2)

    def block(self, k):
        return flip(self.z, k % 2, k // 2)

    def rows(self, turn, block, part):
        return pl.ds(pl.multiple_of(((block * 2 + part) * 2 + turn) * self.each, 16), self.each)

    def core_copy(self, slot):
        return pltpu.make_async_remote_copy(
            src_ref=self.core_out.at[slot], dst_ref=self.core_in.at[slot],
            send_sem=self.core_send.at[slot], recv_sem=self.core_recv.at[slot],
            device_id={"batch": self.sib}, device_id_type=MESH,
        )

    def x_copy(self, k):
        return pltpu.make_async_remote_copy(
            src_ref=self.x_out.at[k], dst_ref=self.x_in.at[k],
            send_sem=self.x_send.at[k], recv_sem=self.x_recv.at[k],
            device_id={"batch": self.across}, device_id_type=MESH,
        )

    def z_copy(self, turn, kind):
        slot = turn * 3 + kind
        return pltpu.make_async_remote_copy(
            src_ref=self.z_out.at[slot], dst_ref=self.z_in.at[slot],
            send_sem=self.z_send.at[slot], recv_sem=self.z_recv.at[slot],
            device_id={"seq": self.block(2 if kind == 2 else 1)}, device_id_type=MESH,
        )

    def to_core(self, turn, slot, block, part):
        self.core_out[turn * 8 + slot] = self.terms[
            self.rows(turn, block, part), self.theirs
        ].astype(BF16)
        self.core_copy(turn * 8 + slot).start()

    def to_x(self, turn, k, block):
        self.core_copy(turn * 8 + k).wait_recv()
        own = self.terms[self.rows(turn, block, 1 - self.x), self.mine]
        total = own + self.core_in[turn * 8 + k].astype(F32)
        self.x_out[turn * 4 + k] = total.astype(BF16)
        self.x_copy(turn * 4 + k).start()

    def start_early(self):
        for turn in range(2):
            self.to_core(turn, self.early_unit, self.early_block, 1 - self.x)
        for turn in range(2):
            self.to_x(turn, self.early_unit, self.early_block)

    def stage(self, turn, k):
        self.core_copy(turn * 8 + 4 + k).wait_recv()
        self.x_copy(turn * 4 + k).wait_recv()
        own = self.terms[self.rows(turn, self.block(k), self.x), self.mine]
        total = own + self.core_in[turn * 8 + 4 + k].astype(F32)
        total = total + self.x_in[turn * 4 + k].astype(F32)
        if k == 2:
            self.z_copy(turn, 0).wait_recv()
            total = total + self.z_in[turn * 3].astype(F32)
        if k == 0:
            self.kept[turn] = total
        else:
            kind = {3: 0, 1: 1, 2: 2}[k]
            self.z_out[turn * 3 + kind] = total.astype(BF16)
            self.z_copy(turn, kind).start()

    def final_copy(self, turn, index, slot, to):
        place = self.final.at[slot, pl.ds(turn * self.each, self.each)]
        return pltpu.make_async_remote_copy(
            src_ref=place, dst_ref=place,
            send_sem=self.f_send.at[turn, index], recv_sem=self.f_recv.at[turn, index],
            device_id={"batch": to}, device_id_type=MESH,
        )

    def gather(self, turn):
        self.z_copy(turn, 1).wait_recv()
        total = self.kept[turn] + self.z_in[turn * 3 + 1].astype(F32)
        self.z_copy(turn, 2).wait_recv()
        total = total + self.z_in[turn * 3 + 2].astype(F32)
        me = self.x * 2 + self.core
        self.final[me, pl.ds(turn * self.each, self.each)] = total.astype(BF16)
        self.final_copy(turn, 0, me, self.across).start()
        self.final_copy(turn, 1, me, self.sib).start()

    def forward(self, turn):
        self.final_copy(turn, 0, self.across, self.across).wait_recv()
        self.final_copy(turn, 2, self.across, self.sib).start()

    def run(self, meanwhile, wgrad_hbm):
        units = (3, 2, 1, 0)
        for turn in range(2):
            for k in units:
                @pl.when(k != self.early_unit)
                def _():
                    self.to_core(turn, k, self.block(k), 1 - self.x)
        for turn in range(2):
            for k in units:
                @pl.when(k != self.early_unit)
                def _():
                    self.to_x(turn, k, self.block(k))
            for k in units:
                self.to_core(turn, 4 + k, self.block(k), self.x)
        meanwhile(CHUNKS - 2)
        self.stage(0, 3)
        self.stage(0, 2)
        meanwhile(CHUNKS - 1)
        self.stage(0, 1)
        self.stage(0, 0)
        self.stage(1, 3)
        self.stage(1, 2)
        self.gather(0)
        self.stage(1, 1)
        self.stage(1, 0)
        self.forward(0)
        self.gather(1)

        me, sib, across = self.x * 2 + self.core, self.sib, self.across
        last = (1 - self.x) * 2 + 1 - self.core

        def out_copy(slot):
            return pltpu.make_async_copy(
                self.final.at[slot], wgrad_hbm.at[slot], self.o_sem.at[slot]
            )

        out_copy(me).start()
        for turn in range(2):
            self.final_copy(turn, 1, sib, sib).wait_recv()
        out_copy(sib).start()
        self.forward(1)
        out_copy(across).start()
        for turn in range(2):
            self.final_copy(turn, 2, last, sib).wait_recv()
        out_copy(last).start()

        for turn in range(2):
            self.final_copy(turn, 0, me, across).wait_send()
            self.final_copy(turn, 1, me, sib).wait_send()
            self.final_copy(turn, 2, across, sib).wait_send()
            for kind in range(3):
                self.z_copy(turn, kind).wait_send()
        for slot in range(16):
            self.core_copy(slot).wait_send()
        for k in range(8):
            self.x_copy(k).wait_send()
        for slot in range(4):
            out_copy(slot).wait()


def flip(value, bit, high):
    low_part, high_part = value % 2, value // 2
    return 2 * (high_part + high - 2 * high_part * high) + low_part + bit - 2 * low_part * bit


def finish(grad_hbm, parts_hbm, grad_out, wgrad_out, grad, parts, wgrad, sems):
    each, half = parts.shape[1:]
    into = pltpu.make_async_copy(grad_hbm, grad, sems.at[0])
    parts_in = pltpu.make_async_copy(parts_hbm, parts, sems.at[1])
    parts_in.start()
    into.start()
    parts_in.wait()
    out = []
    for part in range(2):
        rows = pl.ds(part * each, each)
        for side in range(2):
            wgrad[rows, pl.ds(side * half, half)] = parts[part * 2 + side].astype(F32)
        out.append(pltpu.make_async_copy(wgrad.at[rows], wgrad_out.at[rows], sems.at[3 + part]))
        out[-1].start()
    into.wait()
    out.append(pltpu.make_async_copy(grad, grad_out, sems.at[2]))
    out[-1].start()
    for copy in out:
        copy.wait()


def on_device(seq, batch, head, u1, u2, w1, w2, c1, c2):
    chan, width = u1.shape[1:]
    out_chan = w1.shape[2]
    taps = w1.shape[0]
    total_rows = taps * chan
    factor = 1.0 / math.sqrt(u1.shape[0] * batch * width * seq)
    spans = (DILATION_FIRST // width, DILATION_SECOND // width)
    rows = total_rows // seq
    rows_each, half = rows // 2, out_chan // 2
    early = [
        [
            block for block in range(seq)
            if chan <= (2 * block + part) * rows_each <= 2 * chan - rows_each
        ][:1]
        for part in range(2)
    ]
    reduce = (
        seq == 4 and batch == 4 and rows % 64 == 0 and out_chan % 256 == 0 and all(early)
    )
    early = [blocks[0] for blocks in early] if reduce else None
    vmem = pl.BlockSpec(memory_space=pltpu.VMEM)
    anywhere = pl.BlockSpec(memory_space=pl.ANY)
    dma = pltpu.SemaphoreType.DMA
    scratch = [
        pltpu.VMEM((chan, width), BF16),
        pltpu.VMEM((chan, width), BF16),
        pltpu.VMEM((chan, width), BF16),
        pltpu.VMEM((chan, 128), F32),
        pltpu.VMEM((chan, 128), F32),
        pltpu.VMEM(w1.shape, BF16),
        pltpu.VMEM(w2.shape, BF16),
        pltpu.VMEM((3, chan, width), BF16),
        pltpu.VMEM((3, chan, width), BF16),
        pltpu.VMEM((chan, width), F32),
        pltpu.VMEM((chan, width), F32),
        pltpu.VMEM((1, width), F32),
        pltpu.VMEM((1, width), F32),
        pltpu.VMEM((chan, width), BF16),
        pltpu.VMEM((chan, width // CHUNKS), F32),
        pltpu.VMEM((total_rows, out_chan), F32),
        dma((7 + CHUNKS,)),
        dma((CHUNKS, seq - 1, 3)),
        dma((CHUNKS, seq - 1, 3)),
        dma((CHUNKS, 2)),
        dma((CHUNKS, 2)),
    ]
    if reduce:
        unit = rows_each // 2
        scratch += [
            pltpu.VMEM((16, unit, half), BF16),
            pltpu.VMEM((16, unit, half), BF16),
            pltpu.VMEM((8, unit, half), BF16),
            pltpu.VMEM((8, unit, half), BF16),
            pltpu.VMEM((6, unit, half), BF16),
            pltpu.VMEM((6, unit, half), BF16),
            pltpu.VMEM((2, unit, half), F32),
            pltpu.VMEM((4, rows_each, half), BF16),
            dma((16,)),
            dma((16,)),
            dma((8,)),
            dma((8,)),
            dma((6,)),
            dma((6,)),
            dma((2, 3)),
            dma((2, 3)),
            dma((4,)),
        ]
    grad, wgrad = pl.pallas_call(
        functools.partial(kernel, seq, spans, factor, early),
        out_shape=(
            jax.ShapeDtypeStruct((chan, width), BF16),
            jax.ShapeDtypeStruct((4, rows_each, half), BF16)
            if reduce else jax.ShapeDtypeStruct((total_rows, out_chan), F32),
        ),
        in_specs=[anywhere] * 5 + [vmem, vmem],
        out_specs=(anywhere, anywhere),
        scratch_shapes=scratch,
        compiler_params=pltpu.CompilerParams(
            collective_id=0, has_side_effects=True, vmem_limit_bytes=56 * 1024 * 1024
        ),
        cost_estimate=pl.CostEstimate(
            flops=18 * chan * out_chan * width, bytes_accessed=20_000_000, transcendentals=2 * chan * width
        ),
    )(head[0], u1[0], u2[0], w1, w2, c1, c2)
    if reduce:
        shapes = (
            jax.ShapeDtypeStruct(grad.shape, BF16),
            jax.ShapeDtypeStruct((rows, out_chan), F32),
        )
        grad, wgrad = pl.pallas_call(
            finish,
            out_shape=shapes,
            in_specs=[anywhere, anywhere],
            out_specs=(anywhere, anywhere),
            scratch_shapes=[
                pltpu.VMEM(grad.shape, BF16),
                pltpu.VMEM(wgrad.shape, BF16),
                pltpu.VMEM((rows, out_chan), F32),
                dma((5,)),
            ],
            compiler_params=pltpu.CompilerParams(vmem_limit_bytes=56 * 1024 * 1024),
        )(grad, wgrad)
    else:
        wgrad = lax.psum(lax.psum_scatter(wgrad, "seq", scatter_dimension=0, tiled=True), "batch")
    return grad[None], wgrad


def solution(mesh):
    in_specs = (
        P(("grp", "batch"), "seq", None),
        P(("grp", "batch"), None, "seq"),
        P(("grp", "batch"), None, "seq"),
        P(),
        P(),
        P(),
        P(),
    )
    out_specs = (P(("grp", "batch"), None, "seq"), P(("grp", "seq"), None))
    return jax.shard_map(
        functools.partial(on_device, mesh.shape["seq"], mesh.shape["batch"]),
        mesh=mesh, in_specs=in_specs, out_specs=out_specs, check_vma=False,
    )
```

```python
import functools
import math

import jax
import jax.numpy as jnp
from jax import lax
from jax.experimental import pallas as pl
from jax.experimental.pallas import tpu as pltpu
from jax.sharding import PartitionSpec as P

DILATION_FIRST = 512
DILATION_SECOND = 1024

EPS = 1e-06
SLOPE = math.sqrt(2.0 / math.pi)
CUBIC = 0.044715

F32 = jnp.float32
BF16 = jnp.bfloat16
MESH = pl.DeviceIdType.MESH
CHUNKS = 4
AHEAD = 2
STRIP = 64
BLOCK = 768


def prepare(u_ref, gain_ref, slope_ref, scale_ref, gelu_ref):
    chan, width = u_ref.shape

    def square(step, total):
        rows = pl.ds(pl.multiple_of(step * STRIP, STRIP), STRIP)
        x = u_ref[rows, :].astype(F32)
        return total + jnp.sum(x * x, axis=0, keepdims=True)

    total = lax.fori_loop(0, chan // STRIP, square, jnp.zeros((1, width), F32))
    scale = lax.rsqrt(total / chan + EPS)
    scale_ref[...] = scale

    @pl.loop(0, chan // STRIP)
    def _(step):
        rows = pl.ds(pl.multiple_of(step * STRIP, STRIP), STRIP)
        gain = gain_ref[rows, 0:1]
        a = u_ref[rows, :].astype(F32) * scale * gain
        t = jnp.tanh(SLOPE * (a + CUBIC * a * a * a))
        slope = 0.5 * (1.0 + t) + 0.5 * a * (1.0 - t * t) * SLOPE * (1.0 + 3.0 * CUBIC * a * a)
        slope_ref[rows, :] = slope * gain
        if gelu_ref is not None:
            gelu_ref[rows, :] = (0.5 * a * (1.0 + t)).astype(BF16)


def layer(w_ref, e_ref, has_low, has_up, cols, u_ref, slope_ref, scale_ref, dg_ref, store):
    chan = u_ref.shape[0]
    width = cols.size

    def taps(tap, side, add):
        @pl.loop(0, chan // BLOCK)
        def _(step):
            rows = pl.ds(pl.multiple_of(step * BLOCK, BLOCK), BLOCK)
            part = jnp.dot(w_ref[tap, rows, :], e_ref[side, :, cols], preferred_element_type=F32)
            dg_ref[rows, :] = dg_ref[rows, :] + part if add else part

    taps(1, 1, False)

    @pl.when(has_low)
    def _():
        taps(2, 0, True)

    @pl.when(has_up)
    def _():
        taps(0, 2, True)

    def inner_step(step, total):
        rows = pl.ds(pl.multiple_of(step * STRIP, STRIP), STRIP)
        dn = dg_ref[rows, :] * slope_ref[rows, cols]
        dg_ref[rows, :] = dn
        return total + jnp.sum(dn * u_ref[rows, cols].astype(F32), axis=0, keepdims=True)

    inner = lax.fori_loop(0, chan // STRIP, inner_step, jnp.zeros((1, width), F32)) / chan
    scale = scale_ref[:, cols]
    cubed = scale * scale * scale * inner

    @pl.loop(0, chan // STRIP)
    def _(step):
        rows = pl.ds(pl.multiple_of(step * STRIP, STRIP), STRIP)
        dinput = scale * dg_ref[rows, :] - u_ref[rows, cols].astype(F32) * cubed
        store(rows, (e_ref[1, rows, cols].astype(F32) + dinput).astype(BF16))


def kernel(
    count, spans, factor, early,
    h_ref, u1_hbm, u2_hbm, w1_hbm, w2_hbm, c1_ref, c2_ref,
    grad_hbm, wgrad_hbm,
    u1_ref, u2_ref, grad_ref, gain1, gain2, w1, w2, e, m, slope1, slope2, scale1, scale2, gelu1, dg, terms,
    w_sem, a_send, a_recv, b_send, b_recv, *more,
):
    span_first, span_second = spans
    z = lax.axis_index("seq")
    chan, width = u1_ref.shape
    share = h_ref.shape[0]
    piece = width // CHUNKS

    load2 = pltpu.make_async_copy(w2_hbm, w2, w_sem.at[0])
    load1 = pltpu.make_async_copy(w1_hbm, w1, w_sem.at[1])
    load_u2 = pltpu.make_async_copy(u2_hbm, u2_ref, w_sem.at[2])
    load_u1 = pltpu.make_async_copy(u1_hbm, u1_ref, w_sem.at[3])

    offsets = sorted(range(1, count), key=lambda j: -min(j, count - j))
    barrier = pltpu.get_barrier_semaphore()
    partners = [{"seq": lax.rem(z + j, count)} for j in offsets]
    if early is not None:
        b = lax.axis_index("batch")
        x, core = b // 2, b % 2
        sib, across = x * 2 + 1 - core, (1 - x) * 2 + core
        partners += [{"batch": sib}, {"batch": across}]
    for partner in partners:
        pl.semaphore_signal(barrier, inc=1, device_id=partner, device_id_type=MESH)
    pl.semaphore_wait(barrier, len(partners))

    def valid(side, owner, span):
        if side == 0:
            return owner >= span
        return owner + span < count

    def share_copy(q, j, side, source, dest):
        shift = (side - 1) * span_second
        at = pl.multiple_of((dest + shift) * width, 128) + q * piece
        return pltpu.make_async_remote_copy(
            src_ref=h_ref.at[:, pl.ds(pl.multiple_of(at, 128), piece)],
            dst_ref=e.at[side, pl.ds(pl.multiple_of(source * share, 16), share), pl.ds(q * piece, piece)],
            send_sem=a_send.at[q, j - 1, side],
            recv_sem=a_recv.at[q, j - 1, side],
            device_id={"seq": dest},
            device_id_type=MESH,
        )

    def each_share(q, act, incoming):
        for j in offsets:
            source = lax.rem(z - j + count, count) if incoming else z
            dest = z if incoming else lax.rem(z + j, count)
            for side in (0, 1, 2):
                def go(side=side):
                    act(share_copy(q, j, side, source, dest))
                if side == 1:
                    go()
                else:
                    pl.when(valid(side, dest, span_second))(go)

    for q in range(AHEAD):
        each_share(q, lambda copy: copy.start(), False)

    own = pl.ds(pl.multiple_of(z * share, 16), share)

    def each_own(act):
        for side in (0, 1, 2):
            def keep(side=side):
                at = pl.multiple_of((z + (side - 1) * span_second) * width, 128)
                act(pltpu.make_async_copy(
                    h_ref.at[:, pl.ds(at, width)], e.at[side, own, :], w_sem.at[4 + side]
                ))
            if side == 1:
                keep()
            else:
                pl.when(valid(side, z, span_second))(keep)

    load_u2.start()
    load_u1.start()
    each_own(lambda copy: copy.start())
    load2.start()
    load1.start()
    for gain, row in ((gain1, c1_ref), (gain2, c2_ref)):
        gain[...] = jnp.transpose(jnp.broadcast_to(row[...].reshape(1, chan), (gain.shape[1], chan)))
    load_u2.wait()
    prepare(u2_ref, gain2, slope2, scale2, None)
    load_u1.wait()
    prepare(u1_ref, gain1, slope1, scale1, gelu1)
    load2.wait()
    each_own(lambda copy: copy.wait())

    def border_copy(q, side):
        to = z + span_first if side == 0 else z - span_first
        cols = pl.ds(q * piece, piece)
        return pltpu.make_async_remote_copy(
            src_ref=m.at[1, :, cols],
            dst_ref=m.at[side, :, cols],
            send_sem=b_send.at[q, side // 2],
            recv_sem=b_recv.at[q, side // 2],
            device_id={"seq": to},
            device_id_type=MESH,
        )

    sends_up = z + span_first < count
    sends_down = z >= span_first

    for q in range(CHUNKS):
        each_share(q, lambda copy: copy.wait_recv(), True)
        if q + AHEAD < CHUNKS:
            each_share(q + AHEAD, lambda copy: copy.start(), False)
        cols = pl.ds(q * piece, piece)

        def store_middle(rows, value):
            m[1, rows, cols] = value

        layer(
            w2, e, valid(0, z, span_second), valid(2, z, span_second), cols,
            u2_ref, slope2, scale2, dg, store_middle,
        )

        @pl.when(sends_up)
        def _():
            border_copy(q, 0).start()

        @pl.when(sends_down)
        def _():
            border_copy(q, 2).start()

    def tap_terms(tap, side, cols, add):
        part = lax.dot_general(
            gelu1[:, cols], m[side, :, cols],
            (((1,), (1,)), ((), ())), preferred_element_type=F32,
        ) * factor
        rows = pl.ds(tap * chan, chan)
        terms[rows, :] = terms[rows, :] + part if add else part

    def border_terms(tap, side, has, cols, add):
        @pl.when(has)
        def _():
            tap_terms(tap, side, cols, add)

        if not add:
            @pl.when(jnp.logical_not(has))
            def _():
                terms[pl.ds(tap * chan, chan), :] = jnp.zeros((chan, terms.shape[1]), F32)

    def store_total(cols):
        def store(rows, value):
            grad_ref[rows, cols] = value
        return store

    def result_copy(q):
        cols = pl.ds(q * piece, piece)
        return pltpu.make_async_copy(grad_ref.at[:, cols], grad_hbm.at[:, cols], w_sem.at[7 + q])

    def first_layer(q):
        cols = pl.ds(q * piece, piece)
        layer(
            w1, m, sends_down, sends_up, cols,
            u1_ref, slope1, scale1, dg, store_total(cols),
        )
        result_copy(q).start()

    tap_terms(1, 1, pl.ds(0, width), False)
    if early is not None:
        reduction = Reduction(z, x, core, sib, across, early, terms, more)
        reduction.start_early()
    load1.wait()
    for q in range(CHUNKS):
        pl.when(sends_down)(border_copy(q, 0).wait_recv)
        pl.when(sends_up)(border_copy(q, 2).wait_recv)
        if q < CHUNKS - 2:
            first_layer(q)
        else:
            add = q == CHUNKS - 1
            cols = pl.ds(q * piece, piece) if add else pl.ds(0, (CHUNKS - 1) * piece)
            border_terms(0, 2, sends_up, cols, add)
            border_terms(2, 0, sends_down, cols, add)

    if early is not None:
        reduction.run(first_layer, wgrad_hbm)
    else:
        first_layer(CHUNKS - 2)
        first_layer(CHUNKS - 1)
        terms_out = pltpu.make_async_copy(terms, wgrad_hbm, w_sem.at[0])
        terms_out.start()
        terms_out.wait()
    for q in range(CHUNKS):
        result_copy(q).wait()

    for q in range(CHUNKS):
        each_share(q, lambda copy: copy.wait_send(), False)

        @pl.when(sends_up)
        def _():
            border_copy(q, 0).wait_send()

        @pl.when(sends_down)
        def _():
            border_copy(q, 2).wait_send()


class Reduction:
    def __init__(self, z, x, core, sib, across, early, terms, refs):
        self.z, self.x, self.core, self.sib, self.across = z, x, core, sib, across
        self.terms = terms
        (self.core_out, self.core_in, self.x_out, self.x_in, self.z_out, self.z_in, self.kept, self.final,
         self.core_send, self.core_recv, self.x_send, self.x_recv,
         self.z_send, self.z_recv, self.f_send, self.f_recv, self.o_sem) = refs
        self.each, self.half = self.core_out.shape[1:]
        self.mine = pl.ds(pl.multiple_of(core * self.half, 128), self.half)
        self.theirs = pl.ds(pl.multiple_of((1 - core) * self.half, 128), self.half)
        self.early_block = early[1] + x * (early[0] - early[1])
        self.early_unit = flip(self.early_block, z % 2, z // 2)

    def block(self, k):
        return flip(self.z, k % 2, k // 2)

    def rows(self, turn, block, part):
        return pl.ds(pl.multiple_of(((block * 2 + part) * 2 + turn) * self.each, 16), self.each)

    def core_copy(self, slot):
        return pltpu.make_async_remote_copy(
            src_ref=self.core_out.at[slot], dst_ref=self.core_in.at[slot],
            send_sem=self.core_send.at[slot], recv_sem=self.core_recv.at[slot],
            device_id={"batch": self.sib}, device_id_type=MESH,
        )

    def x_copy(self, k):
        return pltpu.make_async_remote_copy(
            src_ref=self.x_out.at[k], dst_ref=self.x_in.at[k],
            send_sem=self.x_send.at[k], recv_sem=self.x_recv.at[k],
            device_id={"batch": self.across}, device_id_type=MESH,
        )

    def z_copy(self, turn, kind):
        slot = turn * 3 + kind
        return pltpu.make_async_remote_copy(
            src_ref=self.z_out.at[slot], dst_ref=self.z_in.at[slot],
            send_sem=self.z_send.at[slot], recv_sem=self.z_recv.at[slot],
            device_id={"seq": self.block(2 if kind == 2 else 1)}, device_id_type=MESH,
        )

    def to_core(self, turn, slot, block, part):
        self.core_out[turn * 8 + slot] = self.terms[
            self.rows(turn, block, part), self.theirs
        ].astype(BF16)
        self.core_copy(turn * 8 + slot).start()

    def to_x(self, turn, k, block):
        self.core_copy(turn * 8 + k).wait_recv()
        own = self.terms[self.rows(turn, block, 1 - self.x), self.mine]
        total = own + self.core_in[turn * 8 + k].astype(F32)
        self.x_out[turn * 4 + k] = total.astype(BF16)
        self.x_copy(turn * 4 + k).start()

    def start_early(self):
        for turn in range(2):
            self.to_core(turn, self.early_unit, self.early_block, 1 - self.x)
        for turn in range(2):
            self.to_x(turn, self.early_unit, self.early_block)

    def stage(self, turn, k):
        self.core_copy(turn * 8 + 4 + k).wait_recv()
        self.x_copy(turn * 4 + k).wait_recv()
        own = self.terms[self.rows(turn, self.block(k), self.x), self.mine]
        total = own + self.core_in[turn * 8 + 4 + k].astype(F32)
        total = total + self.x_in[turn * 4 + k].astype(F32)
        if k == 2:
            self.z_copy(turn, 0).wait_recv()
            total = total + self.z_in[turn * 3].astype(F32)
        if k == 0:
            self.kept[turn] = total
        else:
            kind = {3: 0, 1: 1, 2: 2}[k]
            self.z_out[turn * 3 + kind] = total.astype(BF16)
            self.z_copy(turn, kind).start()

    def final_copy(self, turn, index, slot, to):
        place = self.final.at[slot, pl.ds(turn * self.each, self.each)]
        return pltpu.make_async_remote_copy(
            src_ref=place, dst_ref=place,
            send_sem=self.f_send.at[turn, index], recv_sem=self.f_recv.at[turn, index],
            device_id={"batch": to}, device_id_type=MESH,
        )

    def gather(self, turn):
        self.z_copy(turn, 1).wait_recv()
        total = self.kept[turn] + self.z_in[turn * 3 + 1].astype(F32)
        self.z_copy(turn, 2).wait_recv()
        total = total + self.z_in[turn * 3 + 2].astype(F32)
        me = self.x * 2 + self.core
        self.final[me, pl.ds(turn * self.each, self.each)] = total.astype(BF16)
        self.final_copy(turn, 0, me, self.across).start()
        self.final_copy(turn, 1, me, self.sib).start()

    def forward(self, turn):
        self.final_copy(turn, 0, self.across, self.across).wait_recv()
        self.final_copy(turn, 2, self.across, self.sib).start()

    def run(self, meanwhile, wgrad_hbm):
        units = (3, 2, 1, 0)
        for turn in range(2):
            for k in units:
                @pl.when(k != self.early_unit)
                def _():
                    self.to_core(turn, k, self.block(k), 1 - self.x)
        for turn in range(2):
            for k in units:
                @pl.when(k != self.early_unit)
                def _():
                    self.to_x(turn, k, self.block(k))
            for k in units:
                self.to_core(turn, 4 + k, self.block(k), self.x)
        meanwhile(CHUNKS - 2)
        self.stage(0, 3)
        self.stage(0, 2)
        meanwhile(CHUNKS - 1)
        self.stage(0, 1)
        self.stage(0, 0)
        self.stage(1, 3)
        self.stage(1, 2)
        self.gather(0)
        self.stage(1, 1)
        self.stage(1, 0)
        self.forward(0)
        self.gather(1)

        me, sib, across = self.x * 2 + self.core, self.sib, self.across
        last = (1 - self.x) * 2 + 1 - self.core

        def out_copy(slot):
            return pltpu.make_async_copy(
                self.final.at[slot], wgrad_hbm.at[slot], self.o_sem.at[slot]
            )

        out_copy(me).start()
        for turn in range(2):
            self.final_copy(turn, 1, sib, sib).wait_recv()
        out_copy(sib).start()
        self.forward(1)
        out_copy(across).start()
        for turn in range(2):
            self.final_copy(turn, 2, last, sib).wait_recv()
        out_copy(last).start()

        for turn in range(2):
            self.final_copy(turn, 0, me, across).wait_send()
            self.final_copy(turn, 1, me, sib).wait_send()
            self.final_copy(turn, 2, across, sib).wait_send()
            for kind in range(3):
                self.z_copy(turn, kind).wait_send()
        for slot in range(16):
            self.core_copy(slot).wait_send()
        for k in range(8):
            self.x_copy(k).wait_send()
        for slot in range(4):
            out_copy(slot).wait()


def flip(value, bit, high):
    low_part, high_part = value % 2, value // 2
    return 2 * (high_part + high - 2 * high_part * high) + low_part + bit - 2 * low_part * bit


def finish(grad_hbm, parts_hbm, grad_out, wgrad_out, grad, parts, wgrad, sems):
    each, half = parts.shape[1:]
    into = pltpu.make_async_copy(grad_hbm, grad, sems.at[0])
    parts_in = pltpu.make_async_copy(parts_hbm, parts, sems.at[1])
    parts_in.start()
    into.start()
    parts_in.wait()
    out = []
    for part in range(2):
        rows = pl.ds(part * each, each)
        for side in range(2):
            wgrad[rows, pl.ds(side * half, half)] = parts[part * 2 + side].astype(F32)
        out.append(pltpu.make_async_copy(wgrad.at[rows], wgrad_out.at[rows], sems.at[3 + part]))
        out[-1].start()
    into.wait()
    out.append(pltpu.make_async_copy(grad, grad_out, sems.at[2]))
    out[-1].start()
    for copy in out:
        copy.wait()


def on_device(seq, batch, head, u1, u2, w1, w2, c1, c2):
    chan, width = u1.shape[1:]
    out_chan = w1.shape[2]
    taps = w1.shape[0]
    total_rows = taps * chan
    factor = 1.0 / math.sqrt(u1.shape[0] * batch * width * seq)
    spans = (DILATION_FIRST // width, DILATION_SECOND // width)
    rows = total_rows // seq
    rows_each, half = rows // 2, out_chan // 2
    early = [
        [
            block for block in range(seq)
            if chan <= (2 * block + part) * rows_each <= 2 * chan - rows_each
        ][:1]
        for part in range(2)
    ]
    reduce = (
        seq == 4 and batch == 4 and rows % 64 == 0 and out_chan % 256 == 0 and all(early)
    )
    early = [blocks[0] for blocks in early] if reduce else None
    vmem = pl.BlockSpec(memory_space=pltpu.VMEM)
    anywhere = pl.BlockSpec(memory_space=pl.ANY)
    dma = pltpu.SemaphoreType.DMA
    scratch = [
        pltpu.VMEM((chan, width), BF16),
        pltpu.VMEM((chan, width), BF16),
        pltpu.VMEM((chan, width), BF16),
        pltpu.VMEM((chan, 128), F32),
        pltpu.VMEM((chan, 128), F32),
        pltpu.VMEM(w1.shape, BF16),
        pltpu.VMEM(w2.shape, BF16),
        pltpu.VMEM((3, chan, width), BF16),
        pltpu.VMEM((3, chan, width), BF16),
        pltpu.VMEM((chan, width), F32),
        pltpu.VMEM((chan, width), F32),
        pltpu.VMEM((1, width), F32),
        pltpu.VMEM((1, width), F32),
        pltpu.VMEM((chan, width), BF16),
        pltpu.VMEM((chan, width // CHUNKS), F32),
        pltpu.VMEM((total_rows, out_chan), F32),
        dma((7 + CHUNKS,)),
        dma((CHUNKS, seq - 1, 3)),
        dma((CHUNKS, seq - 1, 3)),
        dma((CHUNKS, 2)),
        dma((CHUNKS, 2)),
    ]
    if reduce:
        unit = rows_each // 2
        scratch += [
            pltpu.VMEM((16, unit, half), BF16),
            pltpu.VMEM((16, unit, half), BF16),
            pltpu.VMEM((8, unit, half), BF16),
            pltpu.VMEM((8, unit, half), BF16),
            pltpu.VMEM((6, unit, half), BF16),
            pltpu.VMEM((6, unit, half), BF16),
            pltpu.VMEM((2, unit, half), F32),
            pltpu.VMEM((4, rows_each, half), BF16),
            dma((16,)),
            dma((16,)),
            dma((8,)),
            dma((8,)),
            dma((6,)),
            dma((6,)),
            dma((2, 3)),
            dma((2, 3)),
            dma((4,)),
        ]
    grad, wgrad = pl.pallas_call(
        functools.partial(kernel, seq, spans, factor, early),
        out_shape=(
            jax.ShapeDtypeStruct((chan, width), BF16),
            jax.ShapeDtypeStruct((4, rows_each, half), BF16)
            if reduce else jax.ShapeDtypeStruct((total_rows, out_chan), F32),
        ),
        in_specs=[anywhere] * 5 + [vmem, vmem],
        out_specs=(anywhere, anywhere),
        scratch_shapes=scratch,
        compiler_params=pltpu.CompilerParams(
            collective_id=0, has_side_effects=True, vmem_limit_bytes=56 * 1024 * 1024
        ),
        cost_estimate=pl.CostEstimate(
            flops=18 * chan * out_chan * width, bytes_accessed=20_000_000, transcendentals=2 * chan * width
        ),
    )(head[0], u1[0], u2[0], w1, w2, c1, c2)
    if reduce:
        shapes = (
            jax.ShapeDtypeStruct(grad.shape, BF16),
            jax.ShapeDtypeStruct((rows, out_chan), F32),
        )
        grad, wgrad = pl.pallas_call(
            finish,
            out_shape=shapes,
            in_specs=[anywhere, anywhere],
            out_specs=(anywhere, anywhere),
            scratch_shapes=[
                pltpu.VMEM(grad.shape, BF16),
                pltpu.VMEM(wgrad.shape, BF16),
                pltpu.VMEM((rows, out_chan), F32),
                dma((5,)),
            ],
            compiler_params=pltpu.CompilerParams(vmem_limit_bytes=56 * 1024 * 1024),
        )(grad, wgrad)
    else:
        wgrad = lax.psum(lax.psum_scatter(wgrad, "seq", scatter_dimension=0, tiled=True), "batch")
    return grad[None], wgrad


def solution(mesh):
    in_specs = (
        P(("grp", "batch"), "seq", None),
        P(("grp", "batch"), None, "seq"),
        P(("grp", "batch"), None, "seq"),
        P(),
        P(),
        P(),
        P(),
    )
    out_specs = (P(("grp", "batch"), None, "seq"), P(("grp", "seq"), None))
    return jax.shard_map(
        functools.partial(on_device, mesh.shape["seq"], mesh.shape["batch"]),
        mesh=mesh, in_specs=in_specs, out_specs=out_specs, check_vma=False,
    )
```
